128 devices in a mesh: seq: 128 (over x, z, y, core).
Axes of the slice: x: 4, y: 4, z: 4, core: 2. Of those that a mesh axis runs over, the one named last changes fastest.
Arguments:
- queries: bfloat16 [65536, 768], P('seq'), may hold values from -180 to 180
- keys: bfloat16 [65536, 768], P('seq'), may hold values from -6 to 6
- values: bfloat16 [65536, 768], P('seq'), may hold values from -6 to 6
- w_out: bfloat16 [768, 768], replicated, may hold values from -0.21875 to 0.21875
Outputs:
- layer_out: bfloat16 [65536, 768], P('seq')
The draws below stay inside these ranges and needn't reach their ends.
All inputs are finite; a program needn't handle non-finite values.
Results may differ from the reference program's by a relative error of at most 0.0052.
Values may be sent and summed in bfloat16 or wider, within the bound.
A program may use at most 128 MiB of HBM per device.

```python
import jax
import jax.numpy as jnp
from jax import lax

D = 768
HEADS = 12
HD = 64
SEG1 = 512
R2 = 4
R3 = 32
R4 = 256
TOKENS = 65536
SEG2 = 2048
SEG3 = 32768
SEG4 = 65536


def shared_keys(key):
    return jnp.clip(jax.random.normal(key, (TOKENS, D), jnp.float32), -6.0, 6.0)


def draw_keys(key, part):
    base = shared_keys(key)
    return base.astype(jnp.bfloat16)


def draw_queries(key, part):
    key = jax.random.fold_in(key, 5)
    result = 2.5 * jnp.clip(jax.random.normal(key, (TOKENS, D), jnp.float32), -6.0, 6.0)
    return result.astype(jnp.bfloat16)


def shard_levels(rng, shape, shards, smallest, high):
    level, own = 1.0, jax.random.fold_in(rng, 6)
    for dim, shards_of in shards:
        draws = jnp.exp(jax.random.uniform(jax.random.fold_in(own, dim), (shards_of,), jnp.float32, smallest / len(shards), high / len(shards)))
        level = level * jnp.repeat(draws, shape[dim] // shards_of).reshape([-1 if axis == dim else 1 for axis in range(len(shape))])
    return level


def normal_values(own_key, extent, scale, reach, shards=(), held_as=jnp.bfloat16):
    factor_of = shard_levels(own_key, extent, shards, -0.22, 0.18) if shards else 1.0
    array = jax.random.normal(own_key, extent, jnp.float32) * scale * factor_of
    return jnp.minimum(jnp.maximum(array, -reach), reach).astype(held_as)


def setup_inputs(seed: int = 0) -> dict:
    splits = jax.random.split(jax.random.key(seed), 5)
    return {
        "queries": draw_queries(jax.random.fold_in(splits[4], 71), 0),
        "keys": draw_keys(jax.random.fold_in(splits[4], 71), 0),
        "values": normal_values(splits[2], (TOKENS, D), 1.0, 6.0, ((0, 128),)),
        "w_out": normal_values(splits[3], (D, D), D ** -0.5, 0.21875),
    }


def dilated(tensor, dilation):
    blocked = tensor.reshape(tensor.shape[0] // dilation, dilation, HEADS, HD)
    return jnp.stack([blocked[:, head_index % dilation, head_index, :] for head_index in range(HEADS)], axis=1)


def attend(query_block, key_block, value_block):
    groups = HEADS // 4
    scaling = HD ** -0.5

    def one_group(group):
        first_head = group * 4
        query_part = lax.dynamic_slice_in_dim(query_block, first_head, 4, 2).astype(jnp.float32)
        key_part = lax.dynamic_slice_in_dim(key_block, first_head, 4, 2).astype(jnp.float32)
        value_part = lax.dynamic_slice_in_dim(value_block, first_head, 4, 2).astype(jnp.float32)
        scores = jnp.einsum("bqhd,bkhd->bhqk", query_part, key_part) * scaling
        highest = jnp.max(scores, axis=-1)
        weights = jnp.exp(scores - highest[..., None])
        totals = jnp.sum(weights, axis=-1)
        rounded = lax.optimization_barrier(weights.astype(jnp.bfloat16))
        mixed = jnp.einsum("bhqk,bkhd->bqhd", rounded.astype(jnp.float32), value_part)
        return highest, totals, mixed

    highest, totals, mixed = lax.map(one_group, jnp.arange(groups, dtype=jnp.int32))
    batch, rows = query_block.shape[0], query_block.shape[1]
    highest = highest.transpose(1, 3, 0, 2).reshape(batch, rows, HEADS)
    totals = totals.transpose(1, 3, 0, 2).reshape(batch, rows, HEADS)
    mixed = mixed.transpose(1, 2, 0, 3, 4).reshape(batch, rows, HEADS, HD)
    return highest, totals, mixed


def spread(highest, totals, mixed, dilation):
    member = (jnp.arange(HEADS, dtype=jnp.int32)[None, :] % dilation) == jnp.arange(dilation, dtype=jnp.int32)[:, None]
    full_rows = highest.shape[0] * dilation
    high_full = jnp.where(member[None], highest[:, None, :], -1e30).reshape(full_rows, HEADS)
    total_full = jnp.where(member[None], totals[:, None, :], 0.0).reshape(full_rows, HEADS)
    mixed_full = jnp.where(member[None, :, :, None], mixed[:, None], 0.0).reshape(full_rows, HEADS, HD)
    return high_full, total_full, mixed_full


def level(queries, keys, values, dilation, seg_rows):
    query_rows = dilated(queries, dilation)
    key_rows = dilated(keys, dilation)
    value_rows = dilated(values, dilation)
    count = query_rows.shape[0] // seg_rows

    def segment(index):
        offset_rows = index * seg_rows
        query_seg = lax.dynamic_slice_in_dim(query_rows, offset_rows, seg_rows, 0)[None]
        key_seg = lax.dynamic_slice_in_dim(key_rows, offset_rows, seg_rows, 0)[None]
        value_seg = lax.dynamic_slice_in_dim(value_rows, offset_rows, seg_rows, 0)[None]
        highest, totals, mixed = attend(query_seg, key_seg, value_seg)
        return highest[0], totals[0], mixed[0]

    highest, totals, mixed = lax.map(segment, jnp.arange(count, dtype=jnp.int32))
    rows = count * seg_rows
    return spread(highest.reshape(rows, HEADS), totals.reshape(rows, HEADS), mixed.reshape(rows, HEADS, HD), dilation)


def merged(levels):
    running_high, running_total, running_mixed = levels[0]
    for level_high, level_total, level_mixed in levels[1:]:
        newest = jnp.maximum(running_high, level_high)
        old_factor = jnp.exp(running_high - newest)
        new_factor = jnp.exp(level_high - newest)
        running_total = old_factor * running_total + new_factor * level_total
        running_mixed = old_factor[..., None] * running_mixed + new_factor[..., None] * level_mixed
        running_high = newest
    attended = (running_mixed / running_total[..., None]).astype(jnp.bfloat16)
    return attended.reshape(attended.shape[0], HEADS * HD)


def reference(queries, keys, values, w_out):
    levels = [
        level(queries, keys, values, 1, SEG1),
        level(queries, keys, values, R2, SEG2 // R2),
        level(queries, keys, values, R3, SEG3 // R3),
        level(queries, keys, values, R4, SEG4 // R4),
    ]
    attended = merged(levels)
    return jnp.dot(attended, w_out, preferred_element_type=jnp.float32).astype(jnp.bfloat16)
```

```python
import functools

import jax
import jax.numpy as jnp
from jax import lax
from jax.experimental import pallas as pl
from jax.experimental.pallas import tpu as pltpu
from jax.sharding import PartitionSpec as P

ROWS = 512
D = 768
HEADS = 12
HD = 64
GROUPS = 3
NEAR = 128
FAR = 16
REST = NEAR - FAR
WIDE = 2 * HD
NONE = -1e30
F32 = jnp.float32
BF16 = jnp.bfloat16
MESH = pl.DeviceIdType.MESH


T_PAIR, T_CROSS, T_X, T_SIB = 0, 1, 2, 3
P_CROSS, P_X, P_SIB = 4, 5, 6
C_X, C_SIB = 7, 8
D_X, D_SIB = 9, 10
X_SIB = 11
Q_UP, Q_DOWN, Q_FAR = 15, 16, 17
X4_SAME, X4_OTHER = 18, 19
R_DOWN, R_UP, R_FAR = 20, 21, 22
L2_PAIR, L2_SIB, L2_FWD = 23, 26, 29
COPIES = 32


def nt(a, b):
    return lax.dot_general(a, b, (((1,), (1,)), ((), ())), preferred_element_type=F32)


def nn(a, b):
    return jnp.dot(a, b, preferred_element_type=F32)


def iota(shape, dim):
    return lax.broadcasted_iota(jnp.int32, shape, dim)


def one_hot(hit):
    return jnp.where(hit, 1.0, 0.0).astype(BF16)


def kernel(
    q_hbm, k_hbm, v_hbm, w_hbm, out_hbm,
    qbuf, kbuf, vbuf, wbuf, pick, qp, tg, kvr, qg, x4s, x4, rs, rg, rm, att, otmp, mtmp, o1, m1, acc, outbuf,
    local_sem, out_sem, send_sem, recv_sem,
):
    me = lax.axis_index("seq")
    zed = (me >> 3) & 3
    above = (me - (zed << 3)) + (((zed + 1) & 3) << 3)
    below = (me - (zed << 3)) + (((zed + 3) & 3) << 3)
    opposite = me ^ 16
    sib, pair, cross, xpeer, other, other_sib = me ^ 1, me ^ 2, me ^ 6, me ^ 32, me ^ 96, me ^ 97

    loads = []
    for number, (hbm, buf) in enumerate(((k_hbm, kbuf), (v_hbm, vbuf), (q_hbm, qbuf), (w_hbm, wbuf))):
        load = pltpu.make_async_copy(hbm, buf, local_sem.at[number])
        load.start()
        loads.append(load)
    barrier = pltpu.get_barrier_semaphore()
    peers = (sib, pair, cross, xpeer, other, other_sib, above, below)
    for peer in peers:
        pl.semaphore_signal(barrier, inc=1, device_id=(peer,), device_id_type=MESH)

    def copy(number, src, dst, device):
        return pltpu.make_async_remote_copy(
            src_ref=src, dst_ref=dst, send_sem=send_sem.at[number], recv_sem=recv_sem.at[number],
            device_id=(device,), device_id_type=MESH,
        )

    remote = {
        T_PAIR: copy(T_PAIR, tg.at[0], tg.at[1], pair),
        T_CROSS: copy(T_CROSS, tg.at[0], tg.at[4], cross),
        T_X: copy(T_X, tg.at[0], tg.at[8], xpeer),
        T_SIB: copy(T_SIB, tg.at[0], tg.at[2], sib),
        P_CROSS: copy(P_CROSS, tg.at[1], tg.at[5], cross),
        P_X: copy(P_X, tg.at[1], tg.at[9], xpeer),
        P_SIB: copy(P_SIB, tg.at[1], tg.at[3], sib),
        C_X: copy(C_X, tg.at[4], tg.at[12], xpeer),
        C_SIB: copy(C_SIB, tg.at[4], tg.at[6], sib),
        D_X: copy(D_X, tg.at[5], tg.at[13], xpeer),
        D_SIB: copy(D_SIB, tg.at[5], tg.at[7], sib),
        Q_UP: copy(Q_UP, qg.at[0], qg.at[1], above),
        Q_DOWN: copy(Q_DOWN, qg.at[0], qg.at[2], below),
        Q_FAR: copy(Q_FAR, qg.at[1], qg.at[3], above),
        X4_SAME: copy(X4_SAME, x4s, x4.at[0], other),
        X4_OTHER: copy(X4_OTHER, x4s, x4.at[1], other_sib),
        R_DOWN: copy(R_DOWN, rs.at[1], rg.at[2], below),
        R_UP: copy(R_UP, rs.at[2], rg.at[1], above),
        R_FAR: copy(R_FAR, rs.at[3], rg.at[3], opposite),
    }
    for step, slot in enumerate((8, 9, 12, 13)):
        remote[X_SIB + step] = copy(X_SIB + step, tg.at[slot], tg.at[slot + 2], sib)
    for group in range(GROUPS):
        heads = pl.ds(4 * group, 4)
        remote[L2_PAIR + group] = copy(L2_PAIR + group, kvr.at[0, heads], kvr.at[1, heads], pair)
        remote[L2_SIB + group] = copy(L2_SIB + group, kvr.at[0, heads], kvr.at[2, heads], sib)
        remote[L2_FWD + group] = copy(L2_FWD + group, kvr.at[1, heads], kvr.at[3, heads], sib)

    def start(*numbers):
        for number in numbers:
            remote[number].start()

    def arrived(*numbers):
        for number in numbers:
            remote[number].wait_recv()

    place = iota((160, ROWS), 0)
    position = ((place & 1) << 8) + (((place >> 1) & 7) << 5) + (((place >> 4) & 7) << 2)
    column = iota((160, ROWS), 1)
    for r in range(4):
        pick[r] = one_hot(column == position + r)

    lane = iota((NEAR, WIDE), 1)
    low_lanes = lane < HD

    loads[0].wait()
    loads[1].wait()
    for b in range(GROUPS):
        for half in range(2):
            columns = pl.ds(256 * b + 128 * half, 128)
            rows = pick[2 * half : 2 * half + 2, 16 * b : 16 * b + NEAR, :].reshape(2 * NEAR, ROWS)
            both = nn(rows, jnp.concatenate((kbuf[:, columns], vbuf[:, columns]), axis=1))
            for odd in range(2):
                j = 4 * b + 2 * half + odd
                part = both[NEAR * odd : NEAR * odd + NEAR]
                key_part, value_part = part[:, :WIDE], pltpu.roll(part[:, WIDE:], HD, 1)
                packed = jnp.where(low_lanes, *((value_part, key_part) if odd else (key_part, value_part)))
                packed = packed.astype(BF16)
                tg[0, j] = packed[:FAR]
                kvr[0, j] = packed[FAR:]
    pl.semaphore_wait(barrier, len(peers))
    start(T_PAIR, T_CROSS, T_X, T_SIB, L2_PAIR)

    loads[2].wait()
    for b in range(GROUPS):
        rows = pick[:, 16 * b : 16 * b + NEAR, :].reshape(ROWS, ROWS)
        ordered = nn(rows, qbuf[:, 256 * b : 256 * b + 256]) * 0.125
        for r in range(4):
            part = ordered[:, 128 * (r // 2) : 128 * (r // 2) + 128]
            wide_low = iota((ROWS, WIDE), 1) < HD
            part = jnp.where(wide_low, *((0.0, part) if r % 2 else (part, 0.0))).astype(BF16)
            qp[4 * b + r] = part
            qg[0, 4 * b + r] = part[NEAR * r : NEAR * r + FAR]
    start(Q_UP, Q_DOWN, L2_PAIR + 1, L2_PAIR + 2, L2_SIB, L2_SIB + 1, L2_SIB + 2)

    eye = one_hot(iota((WIDE, WIDE), 0) == iota((WIDE, WIDE), 1))

    def level_one(j):
        columns = pl.ds(pl.multiple_of((j >> 1) * WIDE, WIDE), WIDE)
        keys = kbuf[:, columns]
        turned = nt(eye, vbuf[:, columns])
        turned = jnp.where((j & 1) == 1, turned[HD:], turned[:HD])
        left = jnp.concatenate((turned, jnp.ones((HD, ROWS), F32)), axis=0).astype(BF16)
        for part in range(2):
            span = pl.ds(256 * part, 256)
            scores = nt(keys, qp[j, span, :])
            highest = jnp.max(scores, axis=0, keepdims=True)
            weights = jnp.exp(scores - highest).astype(BF16)
            mixed = nn(left, weights)
            att[pl.ds(pl.multiple_of(j * HD, HD), HD), span] = (
                mixed[:HD] * (1.0 / mixed[HD : HD + 1])
            ).astype(BF16)
            otmp[:, span] = mixed
            mtmp[:, span] = jnp.broadcast_to(highest, (8, 256))
        block = pl.ds(pl.multiple_of((j & 3) * NEAR, NEAR), NEAR)
        o1[j] = otmp[:, block]
        m1[j] = mtmp[:, block]

    def level_ones(first, last):
        def step(j, carry):
            level_one(j)
            return carry

        lax.fori_loop(first, last, step, 0)

    def level_two(j):
        keys = jnp.concatenate(
            (tg[0:4, j].reshape(4 * FAR, WIDE), kvr[0:4, j].reshape(4 * REST, WIDE)), axis=0
        )
        turned = nt(eye, keys)
        turned = jnp.where((j & 1) == 1, turned[:HD], turned[HD:])
        left = jnp.concatenate((turned, jnp.ones((HD, ROWS), F32)), axis=0).astype(BF16)
        block = pl.ds(pl.multiple_of((j & 3) * NEAR, NEAR), NEAR)
        scores = nt(keys, qp[j, block, :])
        highest = jnp.max(scores, axis=0, keepdims=True)
        weights = jnp.exp(scores - highest).astype(BF16)
        mixed = nn(left, weights)
        before = m1[j][0:1]
        newest = jnp.maximum(before, highest)
        o1[j] = o1[j] * jnp.exp(before - newest) + mixed * jnp.exp(highest - newest)
        m1[j] = jnp.broadcast_to(newest, (8, NEAR))

    def level_twos(first, last):
        def step(j, carry):
            level_two(j)
            return carry

        lax.fori_loop(first, last, step, 0)

    def compact():
        rows = iota((FAR, 8 * FAR), 0)
        picked = one_hot(iota((FAR, 8 * FAR), 1) == (rows >> 1) * FAR + (rows & 1))
        for j in range(HEADS):
            tiles = jnp.concatenate([tg[slot, j] for slot in (0, 1, 4, 5, 8, 9, 12, 13)], axis=0)
            x4s[j] = nn(picked, tiles).astype(BF16)

    def partials():
        row = iota((4 * FAR, 16 * FAR), 0)
        col = iota((4 * FAR, 16 * FAR), 1)
        bias = jnp.where(((row & 15) < 2) & ((col & 15) < 2), 0.6931471805599453, 0.0).astype(F32)
        member = (iota((4 * FAR, 2 * FAR), 0) & 15) < 2
        low = iota((4 * FAR, WIDE), 1) < HD
        first_half = iota((4 * FAR, WIDE), 1) < HD + HD // 2
        heads = range(HEADS)
        keys3 = [tg[:, j].reshape(16 * FAR, WIDE) for j in heads]
        keys4 = [x4[:, j].reshape(2 * FAR, WIDE) for j in heads]
        queries = [qg[:, j].reshape(4 * FAR, WIDE) for j in heads]
        scores3 = [nt(queries[j], keys3[j]) + bias for j in heads]
        scores4 = [jnp.where(member, nt(queries[j], keys4[j]), NONE) for j in heads]
        highest = [
            jnp.maximum(
                jnp.max(scores3[j], axis=1, keepdims=True), jnp.max(scores4[j], axis=1, keepdims=True)
            )
            for j in heads
        ]
        weights3 = [jnp.exp(scores3[j] - highest[j]) for j in heads]
        weights4 = [jnp.exp(scores4[j] - highest[j]) for j in heads]
        totals = [
            jnp.sum(weights3[j], axis=1, keepdims=True) + jnp.sum(weights4[j], axis=1, keepdims=True)
            for j in heads
        ]
        mixed = [nn(weights3[j].astype(BF16), keys3[j]) + nn(weights4[j].astype(BF16), keys4[j]) for j in heads]
        for j in heads:
            value = mixed[j] * (1.0 / totals[j])
            if j % 2 == 0:
                value = pltpu.roll(value, HD, 1)
            level = highest[j] + jnp.log(totals[j])
            coarse = level.astype(BF16).astype(F32)
            fine = level - coarse
            whole = jnp.where(low, value, jnp.where(first_half, coarse, fine)).astype(BF16)
            for slot in range(4):
                rs[slot, j] = whole[FAR * slot : FAR * slot + FAR]

    def merge_partials():
        rows = HEADS * FAR
        low = iota((rows, WIDE), 1) < HD
        source = iota((WIDE, WIDE), 0)
        gather = one_hot((source == HD) | (source == HD + HD // 2))
        tiles = [rs[0].reshape(rows, WIDE)] + [rg[slot].reshape(rows, WIDE) for slot in (1, 2, 3)]
        levels = [nn(tile, gather) for tile in tiles]
        highest = functools.reduce(jnp.maximum, levels)
        factors = [jnp.exp(level - highest) for level in levels]
        total = functools.reduce(jnp.add, factors)
        value = functools.reduce(jnp.add, [f * t.astype(F32) for f, t in zip(factors, tiles)])
        merged = jnp.where(low, value / total, highest + jnp.log(total))
        rm[...] = merged.reshape(HEADS, FAR, WIDE)

    def finish(j):
        empty = jnp.where(iota((REST, WIDE), 1) < HD, 0.0, NONE).astype(F32)
        far = jnp.concatenate((rm[j], empty), axis=0).T
        level = far[HD : HD + 1]
        before = m1[j][0:1]
        newest = jnp.maximum(before, level)
        old, new = jnp.exp(before - newest), jnp.exp(level - newest)
        whole = o1[j]
        total = whole[HD : HD + 1] * old + new
        value = (whole[:HD] * old + far[:HD] * new) * (1.0 / total)
        att[HD * j : HD * j + HD, NEAR * (j % 4) : NEAR * (j % 4) + NEAR] = value.astype(BF16)

    level_ones(0, 1)
    arrived(T_PAIR)
    start(P_CROSS, P_X, P_SIB)
    level_ones(1, 2)
    arrived(T_CROSS)
    start(C_X, C_SIB)
    arrived(Q_UP)
    start(Q_FAR)
    level_ones(2, 4)
    arrived(P_CROSS)
    start(D_X, D_SIB)
    arrived(T_X, P_X)
    start(X_SIB, X_SIB + 1)
    level_ones(4, 6)
    arrived(L2_PAIR)
    start(L2_FWD)
    arrived(C_X, D_X)
    start(X_SIB + 2, X_SIB + 3)
    compact()
    start(X4_SAME, X4_OTHER)
    level_ones(6, 10)
    arrived(L2_PAIR + 1)
    start(L2_FWD + 1)
    arrived(T_SIB, P_SIB, C_SIB, D_SIB, X_SIB, X_SIB + 1, X_SIB + 2, X_SIB + 3)
    arrived(Q_DOWN, Q_FAR, X4_SAME, X4_OTHER)
    partials()
    start(R_DOWN, R_UP, R_FAR)
    level_ones(10, 12)
    arrived(L2_SIB, L2_FWD)
    level_twos(0, 4)
    arrived(L2_PAIR + 2)
    start(L2_FWD + 2)
    arrived(L2_SIB + 1, L2_FWD + 1)
    level_twos(4, 8)
    arrived(L2_SIB + 2, L2_FWD + 2)
    level_twos(8, 12)
    arrived(R_DOWN, R_UP, R_FAR)
    merge_partials()
    loads[3].wait()
    for b in range(GROUPS):
        for r in range(4):
            finish(4 * b + r)
        spot = iota((ROWS, ROWS), 0)
        index = (
            ((spot & 3) << 7) + (((((spot >> 2) & 7) + (8 - b)) & 7) << 4) + (((spot >> 5) & 7) << 1) + (spot >> 8)
        )
        back = one_hot(iota((ROWS, ROWS), 1) == index)
        natural = nt(back, att[256 * b : 256 * b + 256, :]).astype(BF16)
        term = nn(natural, wbuf[256 * b : 256 * b + 256, :])
        if b == 0:
            acc[...] = term
        elif b == 1:
            acc[...] += term
        else:
            outbuf[...] = (acc[...] + term).astype(BF16)
    store = pltpu.make_async_copy(outbuf, out_hbm, out_sem)
    store.start()
    for number in range(COPIES):
        remote[number].wait_send()
    store.wait()


def body(queries, keys, values, w_out):
    anywhere = pl.BlockSpec(memory_space=pl.ANY)
    scratch = [
        pltpu.VMEM((ROWS, D), BF16),
        pltpu.VMEM((ROWS, D), BF16),
        pltpu.VMEM((ROWS, D), BF16),
        pltpu.VMEM((D, D), BF16),
        pltpu.VMEM((4, 160, ROWS), BF16),
        pltpu.VMEM((HEADS, ROWS, WIDE), BF16),
        pltpu.VMEM((16, HEADS, FAR, WIDE), BF16),
        pltpu.VMEM((4, HEADS, REST, WIDE), BF16),
        pltpu.VMEM((4, HEADS, FAR, WIDE), BF16),
        pltpu.VMEM((HEADS, FAR, WIDE), BF16),
        pltpu.VMEM((2, HEADS, FAR, WIDE), BF16),
        pltpu.VMEM((4, HEADS, FAR, WIDE), BF16),
        pltpu.VMEM((4, HEADS, FAR, WIDE), BF16),
        pltpu.VMEM((HEADS, FAR, WIDE), F32),
        pltpu.VMEM((D, ROWS), BF16),
        pltpu.VMEM((WIDE, ROWS), F32),
        pltpu.VMEM((8, ROWS), F32),
        pltpu.VMEM((HEADS, WIDE, NEAR), F32),
        pltpu.VMEM((HEADS, 8, NEAR), F32),
        pltpu.VMEM((ROWS, D), F32),
        pltpu.VMEM((ROWS, D), BF16),
        pltpu.SemaphoreType.DMA((4,)),
        pltpu.SemaphoreType.DMA,
        pltpu.SemaphoreType.DMA((COPIES,)),
        pltpu.SemaphoreType.DMA((COPIES,)),
    ]
    return pl.pallas_call(
        kernel,
        out_shape=jax.ShapeDtypeStruct((ROWS, D), BF16),
        in_specs=[anywhere] * 4,
        out_specs=anywhere,
        scratch_shapes=scratch,
        compiler_params=pltpu.CompilerParams(
            collective_id=0, has_side_effects=True, vmem_limit_bytes=48 * 1024 * 1024
        ),
        name="dilated_attention",
    )(queries, keys, values, w_out)


def solution(mesh):
    return jax.shard_map(
        body,
        mesh=mesh,
        in_specs=(P("seq", None), P("seq", None), P("seq", None), P()),
        out_specs=P("seq", None),
        check_vma=False,
    )
```

```python
import functools

import jax
import jax.numpy as jnp
from jax import lax
from jax.experimental import pallas as pl
from jax.experimental.pallas import tpu as pltpu
from jax.sharding import PartitionSpec as P

ROWS = 512
D = 768
HEADS = 12
HD = 64
GROUPS = 3
PAIRS = 6
NEAR = 128
FAR = 16
REST = NEAR - FAR
WIDE = 2 * HD
NONE = -1e30
F32 = jnp.float32
BF16 = jnp.bfloat16
MESH = pl.DeviceIdType.MESH


T_PAIR, T_CROSS, T_X, T_SIB = 0, 1, 2, 3
P_CROSS, P_X, P_SIB = 4, 5, 6
C_X, C_SIB = 7, 8
D_X, D_SIB = 9, 10
X_SIB = 11
Q_UP, Q_DOWN, Q_FAR = 15, 16, 17
X4_SAME, X4_OTHER = 18, 19
R_DOWN, R_UP, R_FAR = 20, 21, 22
L2_PAIR, L2_SIB, L2_FWD = 23, 26, 29
COPIES = 32


def nt(a, b):
    return lax.dot_general(a, b, (((1,), (1,)), ((), ())), preferred_element_type=F32)


def nn(a, b):
    return jnp.dot(a, b, preferred_element_type=F32)


def iota(shape, dim):
    return lax.broadcasted_iota(jnp.int32, shape, dim)


def one_hot(hit):
    return jnp.where(hit, 1.0, 0.0).astype(BF16)


def kernel(
    q_hbm, k_hbm, v_hbm, w_hbm, out_hbm,
    qbuf, kbuf, vbuf, wbuf, pick, back, qp, vt, tg, kvr, qg, x4s, x4, rs, rg, rm, att, sa, sb, pa, pb, o1, m1, outbuf,
    local_sem, out_sem, send_sem, recv_sem,
):
    me = lax.axis_index("seq")
    zed = (me >> 3) & 3
    above = (me - (zed << 3)) + (((zed + 1) & 3) << 3)
    below = (me - (zed << 3)) + (((zed + 3) & 3) << 3)
    opposite = me ^ 16
    sib, pair, cross, xpeer, other, other_sib = me ^ 1, me ^ 2, me ^ 6, me ^ 32, me ^ 96, me ^ 97

    loads = []
    for number, (hbm, buf) in enumerate(((k_hbm, kbuf), (v_hbm, vbuf), (q_hbm, qbuf), (w_hbm, wbuf))):
        load = pltpu.make_async_copy(hbm, buf, local_sem.at[number])
        load.start()
        loads.append(load)
    barrier = pltpu.get_barrier_semaphore()
    peers = (sib, pair, cross, xpeer, other, other_sib, above, below)
    for peer in peers:
        pl.semaphore_signal(barrier, inc=1, device_id=(peer,), device_id_type=MESH)

    def copy(number, src, dst, device):
        return pltpu.make_async_remote_copy(
            src_ref=src, dst_ref=dst, send_sem=send_sem.at[number], recv_sem=recv_sem.at[number],
            device_id=(device,), device_id_type=MESH,
        )

    remote = {
        T_PAIR: copy(T_PAIR, tg.at[0], tg.at[1], pair),
        T_CROSS: copy(T_CROSS, tg.at[0], tg.at[4], cross),
        T_X: copy(T_X, tg.at[0], tg.at[8], xpeer),
        T_SIB: copy(T_SIB, tg.at[0], tg.at[2], sib),
        P_CROSS: copy(P_CROSS, tg.at[1], tg.at[5], cross),
        P_X: copy(P_X, tg.at[1], tg.at[9], xpeer),
        P_SIB: copy(P_SIB, tg.at[1], tg.at[3], sib),
        C_X: copy(C_X, tg.at[4], tg.at[12], xpeer),
        C_SIB: copy(C_SIB, tg.at[4], tg.at[6], sib),
        D_X: copy(D_X, tg.at[5], tg.at[13], xpeer),
        D_SIB: copy(D_SIB, tg.at[5], tg.at[7], sib),
        Q_UP: copy(Q_UP, qg.at[0], qg.at[1], above),
        Q_DOWN: copy(Q_DOWN, qg.at[0], qg.at[2], below),
        Q_FAR: copy(Q_FAR, qg.at[1], qg.at[3], above),
        X4_SAME: copy(X4_SAME, x4s, x4.at[0], other),
        X4_OTHER: copy(X4_OTHER, x4s, x4.at[1], other_sib),
        R_DOWN: copy(R_DOWN, rs.at[1], rg.at[2], below),
        R_UP: copy(R_UP, rs.at[2], rg.at[1], above),
        R_FAR: copy(R_FAR, rs.at[3], rg.at[3], opposite),
    }
    for step, slot in enumerate((8, 9, 12, 13)):
        remote[X_SIB + step] = copy(X_SIB + step, tg.at[slot], tg.at[slot + 2], sib)
    for group in range(GROUPS):
        heads = pl.ds(4 * group, 4)
        remote[L2_PAIR + group] = copy(L2_PAIR + group, kvr.at[0, heads], kvr.at[1, heads], pair)
        remote[L2_SIB + group] = copy(L2_SIB + group, kvr.at[0, heads], kvr.at[2, heads], sib)
        remote[L2_FWD + group] = copy(L2_FWD + group, kvr.at[1, heads], kvr.at[3, heads], sib)

    def start(*numbers):
        for number in numbers:
            remote[number].start()

    def arrived(*numbers):
        for number in numbers:
            remote[number].wait_recv()

    place = iota((ROWS, NEAR), 0)
    position = ((place & 1) << 8) + (((place >> 1) & 7) << 5) + (((place >> 4) & 7) << 2) + (place >> 7)
    column = iota((ROWS, NEAR), 1)
    for c in range(4):
        pick[:, NEAR * c : NEAR * c + NEAR] = one_hot(column + NEAR * c == position)

    low_lanes = iota((NEAR, WIDE), 1) < HD

    loads[0].wait()
    loads[1].wait()
    for t in range(PAIRS):
        b, r = t // 2, 2 * (t % 2)
        columns = pl.ds(WIDE * t, WIDE)
        rows = pick[NEAR * r : NEAR * r + 2 * NEAR, :]
        both = nn(rows, jnp.concatenate((kbuf[:, columns], vbuf[:, columns]), axis=1))
        for kind in range(2):
            lanes = slice(WIDE * kind, WIDE * kind + WIDE)
            rows = jnp.where(low_lanes, both[:NEAR, lanes], both[NEAR:, lanes]).astype(BF16)
            tg[0, 2 * t + kind] = rows[FAR * b : FAR * b + FAR]
            if b > 0:
                kvr[0, 2 * t + kind, 0 : FAR * b, :] = rows[: FAR * b]
            kvr[0, 2 * t + kind, FAR * b : REST, :] = rows[FAR * b + FAR :]
    pl.semaphore_wait(barrier, len(peers))
    start(T_PAIR, T_CROSS, T_X, T_SIB, L2_PAIR)

    loads[2].wait()
    wide_low = iota((ROWS, WIDE), 1) < HD
    for b in range(GROUPS):
        ordered = nn(pick[...], qbuf[:, 256 * b : 256 * b + 256]) * 0.125
        for r in range(4):
            part = ordered[:, 128 * (r // 2) : 128 * (r // 2) + 128]
            part = jnp.where(wide_low, *((0.0, part) if r % 2 else (part, 0.0))).astype(BF16)
            qp[4 * b + r] = part
            qg[0, 4 * b + r] = part[NEAR * r + FAR * b : NEAR * r + FAR * b + FAR]
    start(Q_UP, Q_DOWN, L2_PAIR + 1, L2_PAIR + 2, L2_SIB, L2_SIB + 1, L2_SIB + 2)

    eye = one_hot(iota((WIDE, WIDE), 0) == iota((WIDE, WIDE), 1))

    for t in range(PAIRS):
        vt[WIDE * t : WIDE * t + WIDE, :] = nt(eye, vbuf[:, WIDE * t : WIDE * t + WIDE]).astype(BF16)
    ones = jnp.ones((FAR, ROWS), BF16)

    def scores_of(j, part, into):
        columns = pl.ds(pl.multiple_of((j >> 1) * WIDE, WIDE), WIDE)
        span = pl.ds(256 * part, 256)
        scores = nt(kbuf[:, columns], qp[j, span, :])
        into[...] = scores
        m1[j, :, span] = jnp.broadcast_to(jnp.max(scores, axis=0, keepdims=True), (8, 256))

    def weights_of(j, part, scores, into):
        highest = m1[j, 0:1, 256 * part : 256 * part + 256]
        into[...] = jnp.exp(scores[...] - highest).astype(BF16)

    def mixed_of(j, part, weights):
        span = pl.ds(256 * part, 256)
        left = jnp.concatenate((vt[pl.ds(pl.multiple_of(j * HD, HD), HD), :], ones), axis=0)
        mixed = nn(left, weights[...])
        att[pl.ds(pl.multiple_of(j * HD, HD), HD), span] = (mixed[:HD] * (1.0 / mixed[HD : HD + 1])).astype(BF16)
        o1[j, :, span] = mixed

    def level_ones(first, last):
        def step(j, carry):
            weights_of(j, 0, sa, pa)
            scores_of(j, 1, sb)
            mixed_of(jnp.maximum(j - 1, 0), 1, pb)
            weights_of(j, 1, sb, pb)
            scores_of(jnp.minimum(j + 1, HEADS - 1), 0, sa)
            mixed_of(j, 0, pa)
            return carry

        lax.fori_loop(first, last, step, 0)

    def level_two(group):
        heads = [(t, e) for t in (2 * group, 2 * group + 1) for e in range(2)]
        keys, turned, scores, highs, weights = {}, {}, {}, {}, {}

        def whole(entry):
            return jnp.concatenate(
                (tg[0:4, entry].reshape(4 * FAR, WIDE), kvr[0:4, entry].reshape(4 * REST, WIDE)), axis=0
            )

        def prepare(t):
            keys[t] = whole(2 * t)
            turned[t] = nt(eye, whole(2 * t + 1)).astype(BF16)

        def score(t, e):
            j = 2 * t + e
            scores[j] = nt(keys[t], qp[j, NEAR * (j % 4) : NEAR * (j % 4) + NEAR, :])

        def weigh(t, e):
            j = 2 * t + e
            highs[j] = jnp.max(scores[j], axis=0, keepdims=True)
            weights[j] = jnp.exp(scores[j] - highs[j]).astype(BF16)

        def mix(t, e):
            j = 2 * t + e
            mixed = nn(jnp.concatenate((turned[t][HD * e : HD * e + HD], ones), axis=0), weights[j])
            block = pl.ds(NEAR * (j % 4), NEAR)
            before = m1[j, 0:1, block]
            newest = jnp.maximum(before, highs[j])
            o1[j, :, block] = o1[j, :, block] * jnp.exp(before - newest) + mixed * jnp.exp(highs[j] - newest)
            m1[j, :, block] = jnp.broadcast_to(newest, (8, NEAR))

        for i in range(len(heads) + 2):
            if i < len(heads):
                if heads[i][1] == 0:
                    prepare(heads[i][0])
                score(*heads[i])
            if 0 <= i - 1 < len(heads):
                weigh(*heads[i - 1])
            if 0 <= i - 2 < len(heads):
                mix(*heads[i - 2])

    def compact():
        rows = iota((FAR, 8 * FAR), 0)
        picked = one_hot(iota((FAR, 8 * FAR), 1) == (rows >> 1) * FAR + (rows & 1))
        for entry in range(HEADS):
            tiles = jnp.concatenate([tg[slot, entry] for slot in (0, 1, 4, 5, 8, 9, 12, 13)], axis=0)
            x4s[entry] = nn(picked, tiles).astype(BF16)

    def partials():
        row = iota((4 * FAR, 16 * FAR), 0)
        col = iota((4 * FAR, 16 * FAR), 1)
        bias = jnp.where(((row & 15) < 2) & ((col & 15) < 2), 0.6931471805599453, 0.0).astype(F32)
        member = (iota((4 * FAR, 2 * FAR), 0) & 15) < 2
        low = iota((4 * FAR, WIDE), 1) < HD
        first_half = iota((4 * FAR, WIDE), 1) < HD + HD // 2
        heads = range(HEADS)
        far = [tg[:, entry].reshape(16 * FAR, WIDE) for entry in heads]
        off = [x4[:, entry].reshape(2 * FAR, WIDE) for entry in heads]
        keys3, values3 = [far[j - j % 2] for j in heads], [far[j - j % 2 + 1] for j in heads]
        keys4, values4 = [off[j - j % 2] for j in heads], [off[j - j % 2 + 1] for j in heads]
        queries = [qg[:, j].reshape(4 * FAR, WIDE) for j in heads]
        scores3 = [nt(queries[j], keys3[j]) + bias for j in heads]
        scores4 = [jnp.where(member, nt(queries[j], keys4[j]), NONE) for j in heads]
        highest = [
            jnp.maximum(
                jnp.max(scores3[j], axis=1, keepdims=True), jnp.max(scores4[j], axis=1, keepdims=True)
            )
            for j in heads
        ]
        weights3 = [jnp.exp(scores3[j] - highest[j]) for j in heads]
        weights4 = [jnp.exp(scores4[j] - highest[j]) for j in heads]
        totals = [
            jnp.sum(weights3[j], axis=1, keepdims=True) + jnp.sum(weights4[j], axis=1, keepdims=True)
            for j in heads
        ]
        mixed = [nn(weights3[j].astype(BF16), values3[j]) + nn(weights4[j].astype(BF16), values4[j]) for j in heads]
        for j in heads:
            value = mixed[j] * (1.0 / totals[j])
            if j % 2 == 1:
                value = pltpu.roll(value, HD, 1)
            level = highest[j] + jnp.log(totals[j])
            coarse = level.astype(BF16).astype(F32)
            fine = level - coarse
            whole = jnp.where(low, value, jnp.where(first_half, coarse, fine)).astype(BF16)
            for slot in range(4):
                rs[slot, j] = whole[FAR * slot : FAR * slot + FAR]

    def merge_partials():
        rows = HEADS * FAR
        low = iota((rows, WIDE), 1) < HD
        source = iota((WIDE, WIDE), 0)
        gather = one_hot((source == HD) | (source == HD + HD // 2))
        tiles = [rs[0].reshape(rows, WIDE)] + [rg[slot].reshape(rows, WIDE) for slot in (1, 2, 3)]
        levels = [nn(tile, gather) for tile in tiles]
        highest = functools.reduce(jnp.maximum, levels)
        factors = [jnp.exp(level - highest) for level in levels]
        total = functools.reduce(jnp.add, factors)
        value = functools.reduce(jnp.add, [f * t.astype(F32) for f, t in zip(factors, tiles)])
        merged = jnp.where(low, value / total, highest + jnp.log(total))
        rm[...] = merged.reshape(HEADS, FAR, WIDE)

    def finish(j):
        b, r = j // 4, j % 4
        empty = jnp.where(iota((REST, WIDE), 1) < HD, 0.0, NONE).astype(F32)
        rows = (rm[j], empty) if b == 0 else (empty[: FAR * b], rm[j], empty[FAR * b :])
        far = jnp.concatenate(rows, axis=0).T
        block = pl.ds(NEAR * r, NEAR)
        level = far[HD : HD + 1]
        before = m1[j, 0:1, block]
        newest = jnp.maximum(before, level)
        old, new = jnp.exp(before - newest), jnp.exp(level - newest)
        whole = o1[j, :, block]
        total = whole[HD : HD + 1] * old + new
        value = (whole[:HD] * old + far[:HD] * new) * (1.0 / total)
        att[HD * j : HD * j + HD, block] = value.astype(BF16)

    pb[...] = jnp.zeros_like(pb)
    scores_of(0, 0, sa)
    level_ones(0, 1)
    arrived(T_PAIR)
    start(P_CROSS, P_X, P_SIB)
    level_ones(1, 2)
    arrived(T_CROSS)
    start(C_X, C_SIB)
    arrived(Q_UP)
    start(Q_FAR)
    level_ones(2, 4)
    arrived(P_CROSS)
    start(D_X, D_SIB)
    arrived(T_X, P_X)
    start(X_SIB, X_SIB + 1)
    level_ones(4, 6)
    arrived(L2_PAIR)
    start(L2_FWD)
    arrived(C_X, D_X)
    start(X_SIB + 2, X_SIB + 3)
    compact()
    start(X4_SAME, X4_OTHER)
    level_ones(6, 10)
    arrived(L2_PAIR + 1)
    start(L2_FWD + 1)
    arrived(T_SIB, P_SIB, C_SIB, D_SIB, X_SIB, X_SIB + 1, X_SIB + 2, X_SIB + 3)
    arrived(Q_DOWN, Q_FAR, X4_SAME, X4_OTHER)
    partials()
    start(R_DOWN, R_UP, R_FAR)
    level_ones(10, 12)
    mixed_of(HEADS - 1, 1, pb)
    spot = iota((ROWS, NEAR), 0)
    index = ((spot & 3) << 7) + (((spot >> 2) & 7) << 4) + (((spot >> 5) & 7) << 1) + (spot >> 8)
    column = iota((ROWS, NEAR), 1)
    for c in range(4):
        back[:, NEAR * c : NEAR * c + NEAR] = one_hot(column + NEAR * c == index)
    arrived(L2_SIB, L2_FWD)
    level_two(0)
    arrived(L2_PAIR + 2)
    start(L2_FWD + 2)
    arrived(L2_SIB + 1, L2_FWD + 1)
    level_two(1)
    arrived(L2_SIB + 2, L2_FWD + 2)
    level_two(2)
    arrived(R_DOWN, R_UP, R_FAR)
    merge_partials()
    for j in range(HEADS):
        finish(j)
    loads[3].wait()
    natural = nt(back[...], att[...]).astype(BF16)
    outbuf[...] = nn(natural, wbuf[...]).astype(BF16)
    store = pltpu.make_async_copy(outbuf, out_hbm, out_sem)
    store.start()
    for number in range(COPIES):
        remote[number].wait_send()
    store.wait()


def body(queries, keys, values, w_out):
    anywhere = pl.BlockSpec(memory_space=pltpu.HBM)
    scratch = [
        pltpu.VMEM((ROWS, D), BF16),
        pltpu.VMEM((ROWS, D), BF16),
        pltpu.VMEM((ROWS, D), BF16),
        pltpu.VMEM((D, D), BF16),
        pltpu.VMEM((ROWS, ROWS), BF16),
        pltpu.VMEM((ROWS, ROWS), BF16),
        pltpu.VMEM((HEADS, ROWS, WIDE), BF16),
        pltpu.VMEM((D, ROWS), BF16),
        pltpu.VMEM((16, HEADS, FAR, WIDE), BF16),
        pltpu.VMEM((4, HEADS, REST, WIDE), BF16),
        pltpu.VMEM((4, HEADS, FAR, WIDE), BF16),
        pltpu.VMEM((HEADS, FAR, WIDE), BF16),
        pltpu.VMEM((2, HEADS, FAR, WIDE), BF16),
        pltpu.VMEM((4, HEADS, FAR, WIDE), BF16),
        pltpu.VMEM((4, HEADS, FAR, WIDE), BF16),
        pltpu.VMEM((HEADS, FAR, WIDE), F32),
        pltpu.VMEM((D, ROWS), BF16),
        pltpu.VMEM((ROWS, 256), F32),
        pltpu.VMEM((ROWS, 256), F32),
        pltpu.VMEM((ROWS, 256), BF16),
        pltpu.VMEM((ROWS, 256), BF16),
        pltpu.VMEM((HEADS, HD + FAR, ROWS), F32),
        pltpu.VMEM((HEADS, 8, ROWS), F32),
        pltpu.VMEM((ROWS, D), BF16),
        pltpu.SemaphoreType.DMA((4,)),
        pltpu.SemaphoreType.DMA,
        pltpu.SemaphoreType.DMA((COPIES,)),
        pltpu.SemaphoreType.DMA((COPIES,)),
    ]
    return pl.pallas_call(
        kernel,
        out_shape=jax.ShapeDtypeStruct((ROWS, D), BF16),
        in_specs=[anywhere] * 4,
        out_specs=anywhere,
        scratch_shapes=scratch,
        compiler_params=pltpu.CompilerParams(
            collective_id=0, has_side_effects=True, vmem_limit_bytes=53760 * 1024
        ),
        name="dilated_attention",
    )(queries, keys, values, w_out)


def solution(mesh):
    return jax.shard_map(
        body,
        mesh=mesh,
        in_specs=(P("seq", None), P("seq", None), P("seq", None), P()),
        out_specs=P("seq", None),
        check_vma=False,
    )
```

```python
import functools

import jax
import jax.numpy as jnp
from jax import lax
from jax.experimental import pallas as pl
from jax.experimental.pallas import tpu as pltpu
from jax.sharding import PartitionSpec as P

ROWS = 512
D = 768
HEADS = 12
HD = 64
GROUPS = 3
PAIRS = 6
NEAR = 128
FAR = 16
REST = NEAR - FAR
WIDE = 2 * HD
NONE = -1e30
F32 = jnp.float32
BF16 = jnp.bfloat16
MESH = pl.DeviceIdType.MESH


T_SEND = 0
T_FORWARD = 4
Q_SEND = 7
X_SEND = 14
R_SEND = 22
L2_PAIR, L2_SIB, L2_FWD = 29, 32, 35
COPIES = 38


def nt(a, b):
    return lax.dot_general(a, b, (((1,), (1,)), ((), ())), preferred_element_type=F32)


def nn(a, b):
    return jnp.dot(a, b, preferred_element_type=F32)


def iota(shape, dim):
    return lax.broadcasted_iota(jnp.int32, shape, dim)


def one_hot(hit):
    return jnp.where(hit, 1.0, 0.0).astype(BF16)


def kernel(
    q_hbm, k_hbm, v_hbm, w_hbm, out_hbm,
    qbuf, kbuf, vbuf, wbuf, pick, back, qp, vt, tg, kvr, qg, x4s, x4, rs, rg, rm, att, sa, sb, pa, pb, o1, m1, outbuf,
    local_sem, out_sem, send_sem, recv_sem,
):
    me = lax.axis_index("seq")
    zed = (me >> 3) & 3
    sib, pair = me ^ 1, me ^ 2
    base = me - (zed << 3)

    def around(slot):
        return (base + (((zed + slot) & 3) << 3)) ^ ((slot >> 2) << 5)

    def reverse(slot):
        return (slot & 4) + ((4 - slot) & 3)

    loads = []
    for number, (hbm, buf) in enumerate(((k_hbm, kbuf), (v_hbm, vbuf), (q_hbm, qbuf), (w_hbm, wbuf))):
        load = pltpu.make_async_copy(hbm, buf, local_sem.at[number])
        load.start()
        loads.append(load)
    barrier = pltpu.get_barrier_semaphore()
    peers = [sib] + [me ^ (2 * s) for s in (1, 2, 3)] + [around(s) for s in range(1, 8)] + [me ^ (96 + s) for s in range(8)]
    for peer in peers:
        pl.semaphore_signal(barrier, inc=1, device_id=(peer,), device_id_type=MESH)

    def copy(number, src, dst, device):
        return pltpu.make_async_remote_copy(
            src_ref=src, dst_ref=dst, send_sem=send_sem.at[number], recv_sem=recv_sem.at[number],
            device_id=(device,), device_id_type=MESH,
        )

    remote = {}
    for step, (mask, slot) in enumerate(((2, 1), (6, 4), (4, 5), (1, 2))):
        remote[T_SEND + step] = copy(T_SEND + step, tg.at[0], tg.at[slot], me ^ mask)
    for step, slot in enumerate((1, 4, 5)):
        remote[T_FORWARD + step] = copy(T_FORWARD + step, tg.at[slot], tg.at[slot + 2], sib)
    for slot in range(1, 8):
        number = slot - 1
        remote[Q_SEND + number] = copy(Q_SEND + number, qg.at[0], qg.at[reverse(slot)], around(slot))
        remote[R_SEND + number] = copy(R_SEND + number, rs.at[slot], rg.at[reverse(slot)], around(slot))
    for slot in range(8):
        remote[X_SEND + slot] = copy(X_SEND + slot, x4s, x4.at[slot], me ^ (96 + slot))
    for group in range(GROUPS):
        heads = pl.ds(4 * group, 4)
        remote[L2_PAIR + group] = copy(L2_PAIR + group, kvr.at[0, heads], kvr.at[1, heads], pair)
        remote[L2_SIB + group] = copy(L2_SIB + group, kvr.at[0, heads], kvr.at[2, heads], sib)
        remote[L2_FWD + group] = copy(L2_FWD + group, kvr.at[1, heads], kvr.at[3, heads], sib)

    def start(*numbers):
        for number in numbers:
            remote[number].start()

    def arrived(*numbers):
        for number in numbers:
            remote[number].wait_recv()

    place = iota((ROWS, NEAR), 0)
    position = ((place & 1) << 8) + (((place >> 1) & 7) << 5) + (((place >> 4) & 7) << 2) + (place >> 7)
    column = iota((ROWS, NEAR), 1)
    for c in range(4):
        pick[:, NEAR * c : NEAR * c + NEAR] = one_hot(column + NEAR * c == position)

    low_lanes = iota((NEAR, WIDE), 1) < HD

    loads[0].wait()
    loads[1].wait()
    for t in range(PAIRS):
        b, r = t // 2, 2 * (t % 2)
        columns = pl.ds(WIDE * t, WIDE)
        rows = pick[NEAR * r : NEAR * r + 2 * NEAR, :]
        both = nn(rows, jnp.concatenate((kbuf[:, columns], vbuf[:, columns]), axis=1))
        for kind in range(2):
            lanes = slice(WIDE * kind, WIDE * kind + WIDE)
            rows = jnp.where(low_lanes, both[:NEAR, lanes], both[NEAR:, lanes]).astype(BF16)
            tg[0, 2 * t + kind] = rows[FAR * b : FAR * b + FAR]
            if b > 0:
                kvr[0, 2 * t + kind, 0 : FAR * b, :] = rows[: FAR * b]
            kvr[0, 2 * t + kind, FAR * b : REST, :] = rows[FAR * b + FAR :]
    compact = iota((2 * FAR, HEADS * FAR), 0)
    compact = one_hot(iota((2 * FAR, HEADS * FAR), 1) == (compact >> 1) * FAR + (compact & 1))
    x4s[...] = nn(compact, tg[0].reshape(HEADS * FAR, WIDE)).astype(BF16)

    loads[2].wait()
    wide_low = iota((ROWS, WIDE), 1) < HD
    for b in range(GROUPS):
        ordered = nn(pick[...], qbuf[:, 256 * b : 256 * b + 256]) * 0.125
        for r in range(4):
            part = ordered[:, 128 * (r // 2) : 128 * (r // 2) + 128]
            whole = part[NEAR * r + FAR * b : NEAR * r + FAR * b + FAR]
            if r % 2 == 0:
                before = whole
            else:
                qg[0, 2 * b + r // 2] = jnp.where(low_lanes[:FAR], before, whole).astype(BF16)
            qp[4 * b + r] = jnp.where(wide_low, *((0.0, part) if r % 2 else (part, 0.0))).astype(BF16)
    pl.semaphore_wait(barrier, len(peers))
    start(*range(T_SEND, T_SEND + 3), *range(Q_SEND, Q_SEND + 7), *range(X_SEND, X_SEND + 8))
    start(L2_PAIR, L2_PAIR + 1, L2_PAIR + 2, T_SEND + 3, L2_SIB, L2_SIB + 1, L2_SIB + 2)

    eye = one_hot(iota((WIDE, WIDE), 0) == iota((WIDE, WIDE), 1))

    for t in range(PAIRS):
        vt[WIDE * t : WIDE * t + WIDE, :] = nt(eye, vbuf[:, WIDE * t : WIDE * t + WIDE]).astype(BF16)
    ones = jnp.ones((FAR, ROWS), BF16)

    def scores_of(j, part, into):
        columns = pl.ds(pl.multiple_of((j >> 1) * WIDE, WIDE), WIDE)
        span = pl.ds(256 * part, 256)
        scores = nt(kbuf[:, columns], qp[j, span, :])
        into[...] = scores
        m1[j, :, span] = jnp.broadcast_to(jnp.max(scores, axis=0, keepdims=True), (8, 256))

    def weights_of(j, part, scores, into):
        highest = m1[j, 0:1, 256 * part : 256 * part + 256]
        into[...] = jnp.exp(scores[...] - highest).astype(BF16)

    def mixed_of(j, part, weights):
        span = pl.ds(256 * part, 256)
        left = jnp.concatenate((vt[pl.ds(pl.multiple_of(j * HD, HD), HD), :], ones), axis=0)
        mixed = nn(left, weights[...])
        att[pl.ds(pl.multiple_of(j * HD, HD), HD), span] = (mixed[:HD] * (1.0 / mixed[HD : HD + 1])).astype(BF16)
        o1[j, :, span] = mixed

    def level_ones(first, last):
        def step(j, carry):
            weights_of(j, 0, sa, pa)
            scores_of(j, 1, sb)
            mixed_of(jnp.maximum(j - 1, 0), 1, pb)
            weights_of(j, 1, sb, pb)
            scores_of(jnp.minimum(j + 1, HEADS - 1), 0, sa)
            mixed_of(j, 0, pa)
            return carry

        lax.fori_loop(first, last, step, 0)

    def level_two(group):
        heads = [(t, e) for t in (2 * group, 2 * group + 1) for e in range(2)]
        keys, turned, scores, highs, weights = {}, {}, {}, {}, {}

        def whole(entry):
            return jnp.concatenate(
                (tg[0:4, entry].reshape(4 * FAR, WIDE), kvr[0:4, entry].reshape(4 * REST, WIDE)), axis=0
            )

        def prepare(t):
            keys[t] = whole(2 * t)
            turned[t] = nt(eye, whole(2 * t + 1)).astype(BF16)

        def score(t, e):
            j = 2 * t + e
            scores[j] = nt(keys[t], qp[j, NEAR * (j % 4) : NEAR * (j % 4) + NEAR, :])

        def weigh(t, e):
            j = 2 * t + e
            highs[j] = jnp.max(scores[j], axis=0, keepdims=True)
            weights[j] = jnp.exp(scores[j] - highs[j]).astype(BF16)

        def mix(t, e):
            j = 2 * t + e
            mixed = nn(jnp.concatenate((turned[t][HD * e : HD * e + HD], ones), axis=0), weights[j])
            block = pl.ds(NEAR * (j % 4), NEAR)
            before = m1[j, 0:1, block]
            newest = jnp.maximum(before, highs[j])
            o1[j, :, block] = o1[j, :, block] * jnp.exp(before - newest) + mixed * jnp.exp(highs[j] - newest)
            m1[j, :, block] = jnp.broadcast_to(newest, (8, NEAR))

        for i in range(len(heads) + 2):
            if i < len(heads):
                if heads[i][1] == 0:
                    prepare(heads[i][0])
                score(*heads[i])
            if 0 <= i - 1 < len(heads):
                weigh(*heads[i - 1])
            if 0 <= i - 2 < len(heads):
                mix(*heads[i - 2])

    def partials():
        rows, near = 8 * FAR, (8 + 1) * FAR
        order = iota((HEADS * FAR, 8 * 2 * FAR), 0)
        column = iota((HEADS * FAR, 8 * 2 * FAR), 1)
        wanted = ((order & 15) >> 1) * 2 * FAR + (order >> 4) * 2 + (order & 1)
        other = nn(one_hot(column == wanted), x4[...].reshape(8 * 2 * FAR, WIDE)).astype(BF16)
        row, col = iota((near, rows), 0), iota((near, rows), 1)
        own_half = row < rows
        member = (col & 15) < 2
        bias = jnp.where(
            own_half,
            jnp.where(member & ((row & 15) < 2), 0.6931471805599453, 0.0),
            jnp.where(member, 0.0, NONE),
        ).astype(F32)
        low = (iota((rows, WIDE), 1) < HD).astype(F32)
        masks = (low.astype(BF16), (1.0 - low).astype(BF16))
        ones = jnp.ones((FAR, near), BF16)
        pairs, heads = range(PAIRS), range(HEADS)

        def whole(entry):
            return jnp.concatenate(
                (tg[:, entry].reshape(rows, WIDE), other[FAR * entry : FAR * entry + FAR]), axis=0
            )

        keys = [whole(2 * t) for t in pairs]
        turned = [nt(eye, whole(2 * t + 1)).astype(BF16) for t in pairs]
        queries = [qg[:, t].reshape(rows, WIDE) for t in pairs]
        scores = [nt(keys[j // 2], queries[j // 2] * masks[j % 2]) + bias for j in heads]
        highest = [jnp.max(scores[j], axis=0, keepdims=True) for j in heads]
        weights = [jnp.exp(scores[j] - highest[j]).astype(BF16) for j in heads]
        mixed = [
            nn(jnp.concatenate((turned[j // 2][HD * (j % 2) : HD * (j % 2) + HD], ones), axis=0), weights[j])
            for j in heads
        ]
        totals = [mixed[j][HD : HD + 1] for j in heads]
        values = [(mixed[j][:HD] * (1.0 / totals[j])).astype(BF16) for j in heads]
        for t in pairs:
            both = jnp.concatenate((values[2 * t], values[2 * t + 1]), axis=0)
            rs[:, t] = nt(eye, both).astype(BF16).reshape(8, FAR, WIDE)
        levels = [highest[j] + jnp.log(totals[j]) for j in heads]
        levels = jnp.concatenate(levels + [jnp.zeros((4, rows), F32)], axis=0)
        coarse = levels.astype(BF16)
        fine = (levels - coarse.astype(F32)).astype(BF16)
        stacked = jnp.concatenate((coarse, fine, jnp.zeros((WIDE - 2 * FAR, rows), BF16)), axis=0)
        rs[:, PAIRS] = nt(eye, stacked).astype(BF16).reshape(8, FAR, WIDE)

    def merge_partials():
        source, lane = iota((WIDE, D), 0), iota((WIDE, D), 1)
        gather = one_hot(((source & 15) == (lane >> 6)) & (source < 2 * FAR))
        rs_own = rs[0]
        tiles = [rs_own] + [rg[slot] for slot in range(1, 8)]
        values = [jnp.concatenate([tile[t] for t in range(PAIRS)], axis=1).astype(F32) for tile in tiles]
        levels = nn(jnp.concatenate([tile[PAIRS] for tile in tiles], axis=0), gather)
        levels = [levels[FAR * slot : FAR * slot + FAR] for slot in range(8)]
        highest = functools.reduce(jnp.maximum, levels)
        factors = [jnp.exp(level - highest) for level in levels]
        total = functools.reduce(jnp.add, factors)
        value = functools.reduce(jnp.add, [f * v for f, v in zip(factors, values)]) / total
        level = highest + jnp.log(total)
        coarse = level.astype(BF16)
        fine = (level - coarse.astype(F32)).astype(BF16)
        value = value.astype(BF16)
        column = iota((WIDE, NEAR), 1)
        for t in range(PAIRS):
            b = t // 2
            lanes = slice(WIDE * t, WIDE * t + WIDE)

            def spread(rows):
                empty = jnp.zeros((REST, WIDE), BF16)
                rows = (rows, empty) if b == 0 else (empty[: FAR * b], rows, empty[FAR * b :])
                return nt(eye, jnp.concatenate(rows, axis=0))

            rm[2 * t] = spread(value[:, lanes])
            rm[2 * t + 1] = jnp.where(
                (column >> 4) == b, spread(coarse[:, lanes]) + spread(fine[:, lanes]), NONE
            )

    def finish(j):
        r, rows = j % 4, HD * (j % 2)
        block = pl.ds(NEAR * r, NEAR)
        level = rm[j - j % 2 + 1, rows : rows + 1, :]
        before = m1[j, 0:1, block]
        newest = jnp.maximum(before, level)
        old, new = jnp.exp(before - newest), jnp.exp(level - newest)
        whole = o1[j, :, block]
        total = whole[HD : HD + 1] * old + new
        value = (whole[:HD] * old + rm[j - j % 2, rows : rows + HD, :] * new) * (1.0 / total)
        att[HD * j : HD * j + HD, block] = value.astype(BF16)

    pb[...] = jnp.zeros_like(pb)
    scores_of(0, 0, sa)
    level_ones(0, 4)
    arrived(T_SEND, T_SEND + 1, T_SEND + 2)
    start(T_FORWARD, T_FORWARD + 1, T_FORWARD + 2)
    level_ones(4, 6)
    arrived(T_SEND + 3, *range(T_FORWARD, T_FORWARD + 3), *range(Q_SEND, Q_SEND + 7), *range(X_SEND, X_SEND + 8))
    partials()
    start(*range(R_SEND, R_SEND + 7))
    arrived(L2_PAIR)
    start(L2_FWD)
    level_ones(6, 9)
    arrived(L2_PAIR + 1)
    start(L2_FWD + 1)
    level_ones(9, 12)
    mixed_of(HEADS - 1, 1, pb)
    spot = iota((ROWS, NEAR), 0)
    index = ((spot & 3) << 7) + (((spot >> 2) & 7) << 4) + (((spot >> 5) & 7) << 1) + (spot >> 8)
    column = iota((ROWS, NEAR), 1)
    for c in range(4):
        back[:, NEAR * c : NEAR * c + NEAR] = one_hot(column + NEAR * c == index)
    arrived(L2_SIB, L2_FWD)
    level_two(0)
    arrived(L2_PAIR + 2)
    start(L2_FWD + 2)
    arrived(L2_SIB + 1, L2_FWD + 1)
    level_two(1)
    arrived(L2_SIB + 2, L2_FWD + 2)
    level_two(2)
    arrived(*range(R_SEND, R_SEND + 7))
    merge_partials()
    for j in range(HEADS):
        finish(j)
    loads[3].wait()
    natural = nt(back[...], att[...]).astype(BF16)
    outbuf[...] = nn(natural, wbuf[...]).astype(BF16)
    store = pltpu.make_async_copy(outbuf, out_hbm, out_sem)
    store.start()
    for number in range(COPIES):
        remote[number].wait_send()
    store.wait()


def body(queries, keys, values, w_out):
    anywhere = pl.BlockSpec(memory_space=pltpu.HBM)
    scratch = [
        pltpu.VMEM((ROWS, D), BF16),
        pltpu.VMEM((ROWS, D), BF16),
        pltpu.VMEM((ROWS, D), BF16),
        pltpu.VMEM((D, D), BF16),
        pltpu.VMEM((ROWS, ROWS), BF16),
        pltpu.VMEM((ROWS, ROWS), BF16),
        pltpu.VMEM((HEADS, ROWS, WIDE), BF16),
        pltpu.VMEM((D, ROWS), BF16),
        pltpu.VMEM((8, HEADS, FAR, WIDE), BF16),
        pltpu.VMEM((4, HEADS, REST, WIDE), BF16),
        pltpu.VMEM((8, PAIRS, FAR, WIDE), BF16),
        pltpu.VMEM((2 * FAR, WIDE), BF16),
        pltpu.VMEM((8, 2 * FAR, WIDE), BF16),
        pltpu.VMEM((8, PAIRS + 1, FAR, WIDE), BF16),
        pltpu.VMEM((8, PAIRS + 1, FAR, WIDE), BF16),
        pltpu.VMEM((HEADS, WIDE, NEAR), F32),
        pltpu.VMEM((D, ROWS), BF16),
        pltpu.VMEM((ROWS, 256), F32),
        pltpu.VMEM((ROWS, 256), F32),
        pltpu.VMEM((ROWS, 256), BF16),
        pltpu.VMEM((ROWS, 256), BF16),
        pltpu.VMEM((HEADS, HD + FAR, ROWS), F32),
        pltpu.VMEM((HEADS, 8, ROWS), F32),
        pltpu.VMEM((ROWS, D), BF16),
        pltpu.SemaphoreType.DMA((4,)),
        pltpu.SemaphoreType.DMA,
        pltpu.SemaphoreType.DMA((COPIES,)),
        pltpu.SemaphoreType.DMA((COPIES,)),
    ]
    return pl.pallas_call(
        kernel,
        out_shape=jax.ShapeDtypeStruct((ROWS, D), BF16),
        in_specs=[anywhere] * 4,
        out_specs=anywhere,
        scratch_shapes=scratch,
        compiler_params=pltpu.CompilerParams(
            collective_id=0, has_side_effects=True, vmem_limit_bytes=53760 * 1024
        ),
        name="dilated_attention",
    )(queries, keys, values, w_out)


def solution(mesh):
    return jax.shard_map(
        body,
        mesh=mesh,
        in_specs=(P("seq", None), P("seq", None), P("seq", None), P()),
        out_specs=P("seq", None),
        check_vma=False,
    )
```

```python
import functools

import jax
import jax.numpy as jnp
from jax import lax
from jax.experimental import pallas as pl
from jax.experimental.pallas import tpu as pltpu
from jax.sharding import PartitionSpec as P

ROWS = 512
D = 768
HEADS = 12
HD = 64
GROUPS = 3
PAIRS = 6
NEAR = 128
FAR = 16
REST = NEAR - FAR
WIDE = 2 * HD
NONE = -1e30
F32 = jnp.float32
BF16 = jnp.bfloat16
MESH = pl.DeviceIdType.MESH


T_SEND = 0
T_FORWARD = 4
Q_SEND = 7
X_SEND = 14
R_SEND = 22
L2_SIB, L2_PAIR, L2_FWD = 29, 30, 34
COPIES = 38
CHUNKS = ((0, 2), (2, 4), (4, 5), (5, 6))


def nt(a, b):
    return lax.dot_general(a, b, (((1,), (1,)), ((), ())), preferred_element_type=F32)


def nn(a, b):
    return jnp.dot(a, b, preferred_element_type=F32)


def iota(shape, dim):
    return lax.broadcasted_iota(jnp.int32, shape, dim)


def one_hot(hit):
    return jnp.where(hit, 1.0, 0.0).astype(BF16)


def kernel(
    q_hbm, k_hbm, v_hbm, w_hbm, out_ref,
    qbuf, kbuf, vbuf, wbuf, pick, back, qp, vt, tg, kvr, qg, x4s, x4, rs, rg, rm, att, sa, sb, pa, pb, o1, m1,
    local_sem, send_sem, recv_sem,
):
    me = lax.axis_index("seq")
    zed = (me >> 3) & 3
    sib, pair = me ^ 1, me ^ 2
    base = me - (zed << 3)

    def around(slot):
        return (base + (((zed + slot) & 3) << 3)) ^ ((slot >> 2) << 5)

    def reverse(slot):
        return (slot & 4) + ((4 - slot) & 3)

    loads = []
    for number, (hbm, buf) in enumerate(((k_hbm, kbuf), (v_hbm, vbuf), (q_hbm, qbuf), (w_hbm, wbuf))):
        load = pltpu.make_async_copy(hbm, buf, local_sem.at[number])
        load.start()
        loads.append(load)
    barrier = pltpu.get_barrier_semaphore()
    peers = [sib] + [me ^ (2 * s) for s in (1, 2, 3)] + [around(s) for s in range(1, 8)] + [me ^ (96 + s) for s in range(8)]
    for peer in peers:
        pl.semaphore_signal(barrier, inc=1, device_id=(peer,), device_id_type=MESH)

    def copy(number, src, dst, device):
        return pltpu.make_async_remote_copy(
            src_ref=src, dst_ref=dst, send_sem=send_sem.at[number], recv_sem=recv_sem.at[number],
            device_id=(device,), device_id_type=MESH,
        )

    remote = {}
    for step, (mask, slot) in enumerate(((2, 1), (6, 4), (4, 5), (1, 2))):
        remote[T_SEND + step] = copy(T_SEND + step, tg.at[0], tg.at[slot], me ^ mask)
    for step, slot in enumerate((1, 4, 5)):
        remote[T_FORWARD + step] = copy(T_FORWARD + step, tg.at[slot], tg.at[slot + 2], sib)
    for slot in range(1, 8):
        number = slot - 1
        remote[Q_SEND + number] = copy(Q_SEND + number, qg.at[0], qg.at[reverse(slot)], around(slot))
        remote[R_SEND + number] = copy(R_SEND + number, rs.at[slot], rg.at[reverse(slot)], around(slot))
    for slot in range(8):
        remote[X_SEND + slot] = copy(X_SEND + slot, x4s, x4.at[slot], me ^ (96 + slot))
    remote[L2_SIB] = copy(L2_SIB, kvr.at[0], kvr.at[2], sib)
    for number, (first, last) in enumerate(CHUNKS):
        entries = pl.ds(2 * first, 2 * (last - first))
        remote[L2_PAIR + number] = copy(L2_PAIR + number, kvr.at[0, entries], kvr.at[1, entries], pair)
        remote[L2_FWD + number] = copy(L2_FWD + number, kvr.at[1, entries], kvr.at[3, entries], sib)

    def start(*numbers):
        for number in numbers:
            remote[number].start()

    def arrived(*numbers):
        for number in numbers:
            remote[number].wait_recv()

    place = iota((ROWS, NEAR), 0)
    position = ((place & 1) << 8) + (((place >> 1) & 7) << 5) + (((place >> 4) & 7) << 2) + (place >> 7)
    column = iota((ROWS, NEAR), 1)
    for c in range(4):
        pick[:, NEAR * c : NEAR * c + NEAR] = one_hot(column + NEAR * c == position)

    low_lanes = iota((NEAR, WIDE), 1) < HD

    loads[0].wait()
    loads[1].wait()
    for t in range(PAIRS):
        b, r = t // 2, 2 * (t % 2)
        columns = pl.ds(WIDE * t, WIDE)
        rows = pick[NEAR * r : NEAR * r + 2 * NEAR, :]
        both = nn(rows, jnp.concatenate((kbuf[:, columns], vbuf[:, columns]), axis=1))
        for kind in range(2):
            lanes = slice(WIDE * kind, WIDE * kind + WIDE)
            rows = jnp.where(low_lanes, both[:NEAR, lanes], both[NEAR:, lanes]).astype(BF16)
            tg[0, 2 * t + kind] = rows[FAR * b : FAR * b + FAR]
            if b > 0:
                kvr[0, 2 * t + kind, 0 : FAR * b, :] = rows[: FAR * b]
            kvr[0, 2 * t + kind, FAR * b : REST, :] = rows[FAR * b + FAR :]
    compact = iota((2 * FAR, HEADS * FAR), 0)
    compact = one_hot(iota((2 * FAR, HEADS * FAR), 1) == (compact >> 1) * FAR + (compact & 1))
    x4s[...] = nn(compact, tg[0].reshape(HEADS * FAR, WIDE)).astype(BF16)

    loads[2].wait()
    wide_low = iota((ROWS, WIDE), 1) < HD
    for b in range(GROUPS):
        ordered = nn(pick[...], qbuf[:, 256 * b : 256 * b + 256]) * 0.125
        for r in range(4):
            part = ordered[:, 128 * (r // 2) : 128 * (r // 2) + 128]
            whole = part[NEAR * r + FAR * b : NEAR * r + FAR * b + FAR]
            if r % 2 == 0:
                before = whole
            else:
                qg[0, 2 * b + r // 2] = jnp.where(low_lanes[:FAR], before, whole).astype(BF16)
            qp[4 * b + r] = jnp.where(wide_low, *((0.0, part) if r % 2 else (part, 0.0))).astype(BF16)
    eye = one_hot(iota((WIDE, WIDE), 0) == iota((WIDE, WIDE), 1))
    for t in range(PAIRS):
        vt[WIDE * t : WIDE * t + WIDE, :] = nt(eye, vbuf[:, WIDE * t : WIDE * t + WIDE]).astype(BF16)
    ones = jnp.ones((FAR, ROWS), BF16)

    pl.semaphore_wait(barrier, len(peers))
    start(*range(T_SEND, T_SEND + 3), *range(Q_SEND, Q_SEND + 7), *range(X_SEND, X_SEND + 8))
    start(*range(L2_PAIR, L2_PAIR + 4), T_SEND + 3, L2_SIB)


    def scores_of(j, part, into):
        columns = pl.ds(pl.multiple_of((j >> 1) * WIDE, WIDE), WIDE)
        span = pl.ds(256 * part, 256)
        queries = qp[j, span, :]
        highest = None
        for c in range(4):
            scores = nt(kbuf[NEAR * c : NEAR * c + NEAR, columns], queries)
            into[NEAR * c : NEAR * c + NEAR, :] = scores
            top = jnp.max(scores.reshape(16, 8, 256), axis=0)
            highest = top if highest is None else jnp.maximum(highest, top)
        m1[j, :, span] = jnp.broadcast_to(jnp.max(highest, axis=0, keepdims=True), (8, 256))

    def weights_of(j, part, scores, into):
        highest = m1[j, 0:1, 256 * part : 256 * part + 256]
        for c in range(4):
            rows = slice(NEAR * c, NEAR * c + NEAR)
            into[rows, :] = jnp.exp(scores[rows, :] - highest).astype(BF16)

    def mixed_of(j, part, weights):
        span = pl.ds(256 * part, 256)
        left = jnp.concatenate((vt[pl.ds(pl.multiple_of(j * HD, HD), HD), :], ones), axis=0)
        mixed = nn(left, weights[...])
        att[pl.ds(pl.multiple_of(j * HD, HD), HD), span] = (mixed[:HD] * (1.0 / mixed[HD : HD + 1])).astype(BF16)
        o1[j, :, span] = mixed

    def level_ones(first, last):
        def step(j, carry):
            weights_of(j, 0, sa, pa)
            scores_of(j, 1, sb)
            mixed_of(jnp.maximum(j - 1, 0), 1, pb)
            weights_of(j, 1, sb, pb)
            scores_of(jnp.minimum(j + 1, HEADS - 1), 0, sa)
            mixed_of(j, 0, pa)
            return carry

        lax.fori_loop(first, last, step, 0)

    def level_two(chunk):
        heads = [(t, e) for t in range(*CHUNKS[chunk]) for e in range(2)]
        keys, turned, scores, highs, weights = {}, {}, {}, {}, {}

        def whole(entry):
            return jnp.concatenate(
                (tg[0:4, entry].reshape(4 * FAR, WIDE), kvr[0:4, entry].reshape(4 * REST, WIDE)), axis=0
            )

        def prepare(t):
            keys[t] = whole(2 * t)
            turned[t] = nt(eye, whole(2 * t + 1)).astype(BF16)

        def score(t, e):
            j = 2 * t + e
            scores[j] = nt(keys[t], qp[j, NEAR * (j % 4) : NEAR * (j % 4) + NEAR, :])

        def weigh(t, e):
            j = 2 * t + e
            highs[j] = jnp.max(scores[j], axis=0, keepdims=True)
            weights[j] = jnp.exp(scores[j] - highs[j]).astype(BF16)

        def mix(t, e):
            j = 2 * t + e
            mixed = nn(jnp.concatenate((turned[t][HD * e : HD * e + HD], ones), axis=0), weights[j])
            block = pl.ds(NEAR * (j % 4), NEAR)
            before = m1[j, 0:1, block]
            newest = jnp.maximum(before, highs[j])
            o1[j, :, block] = o1[j, :, block] * jnp.exp(before - newest) + mixed * jnp.exp(highs[j] - newest)
            m1[j, :, block] = jnp.broadcast_to(newest, (8, NEAR))

        for i in range(len(heads) + 2):
            if i < len(heads):
                if heads[i][1] == 0:
                    prepare(heads[i][0])
                score(*heads[i])
            if 0 <= i - 1 < len(heads):
                weigh(*heads[i - 1])
            if 0 <= i - 2 < len(heads):
                mix(*heads[i - 2])

    def partials():
        rows, near = 8 * FAR, (8 + 1) * FAR
        order = iota((HEADS * FAR, 8 * 2 * FAR), 0)
        column = iota((HEADS * FAR, 8 * 2 * FAR), 1)
        wanted = ((order & 15) >> 1) * 2 * FAR + (order >> 4) * 2 + (order & 1)
        other = nn(one_hot(column == wanted), x4[...].reshape(8 * 2 * FAR, WIDE)).astype(BF16)
        row, col = iota((near, rows), 0), iota((near, rows), 1)
        own_half = row < rows
        member = (col & 15) < 2
        bias = jnp.where(
            own_half,
            jnp.where(member & ((row & 15) < 2), 0.6931471805599453, 0.0),
            jnp.where(member, 0.0, NONE),
        ).astype(F32)
        low = (iota((rows, WIDE), 1) < HD).astype(F32)
        masks = (low.astype(BF16), (1.0 - low).astype(BF16))
        ones = jnp.ones((FAR, near), BF16)
        pairs, heads = range(PAIRS), range(HEADS)

        def whole(entry):
            return jnp.concatenate(
                (tg[:, entry].reshape(rows, WIDE), other[FAR * entry : FAR * entry + FAR]), axis=0
            )

        keys = [whole(2 * t) for t in pairs]
        turned = [nt(eye, whole(2 * t + 1)).astype(BF16) for t in pairs]
        queries = [qg[:, t].reshape(rows, WIDE) for t in pairs]
        scores = [nt(keys[j // 2], queries[j // 2] * masks[j % 2]) + bias for j in heads]
        highest = [jnp.max(scores[j], axis=0, keepdims=True) for j in heads]
        weights = [jnp.exp(scores[j] - highest[j]).astype(BF16) for j in heads]
        mixed = [
            nn(jnp.concatenate((turned[j // 2][HD * (j % 2) : HD * (j % 2) + HD], ones), axis=0), weights[j])
            for j in heads
        ]
        totals = [mixed[j][HD : HD + 1] for j in heads]
        values = [(mixed[j][:HD] * (1.0 / totals[j])).astype(BF16) for j in heads]
        for t in pairs:
            both = jnp.concatenate((values[2 * t], values[2 * t + 1]), axis=0)
            rs[:, t] = nt(eye, both).astype(BF16).reshape(8, FAR, WIDE)
        levels = [highest[j] + jnp.log(totals[j]) for j in heads]
        levels = jnp.concatenate(levels + [jnp.zeros((4, rows), F32)], axis=0)
        coarse = levels.astype(BF16)
        fine = (levels - coarse.astype(F32)).astype(BF16)
        stacked = jnp.concatenate((coarse, fine, jnp.zeros((WIDE - 2 * FAR, rows), BF16)), axis=0)
        rs[:, PAIRS] = nt(eye, stacked).astype(BF16).reshape(8, FAR, WIDE)

    def merge_partials():
        source, lane = iota((WIDE, D), 0), iota((WIDE, D), 1)
        gather = one_hot(((source & 15) == (lane >> 6)) & (source < 2 * FAR))
        rs_own = rs[0]
        tiles = [rs_own] + [rg[slot] for slot in range(1, 8)]
        values = [jnp.concatenate([tile[t] for t in range(PAIRS)], axis=1).astype(F32) for tile in tiles]
        levels = nn(jnp.concatenate([tile[PAIRS] for tile in tiles], axis=0), gather)
        levels = [levels[FAR * slot : FAR * slot + FAR] for slot in range(8)]
        highest = functools.reduce(jnp.maximum, levels)
        factors = [jnp.exp(level - highest) for level in levels]
        total = functools.reduce(jnp.add, factors)
        value = functools.reduce(jnp.add, [f * v for f, v in zip(factors, values)]) / total
        level = highest + jnp.log(total)
        coarse = level.astype(BF16)
        fine = (level - coarse.astype(F32)).astype(BF16)
        value = value.astype(BF16)
        column = iota((WIDE, NEAR), 1)
        for t in range(PAIRS):
            b = t // 2
            lanes = slice(WIDE * t, WIDE * t + WIDE)

            def spread(rows):
                empty = jnp.zeros((REST, WIDE), BF16)
                rows = (rows, empty) if b == 0 else (empty[: FAR * b], rows, empty[FAR * b :])
                return nt(eye, jnp.concatenate(rows, axis=0))

            rm[2 * t] = spread(value[:, lanes])
            rm[2 * t + 1] = jnp.where(
                (column >> 4) == b, spread(coarse[:, lanes]) + spread(fine[:, lanes]), NONE
            )

    def finish(j):
        r, rows = j % 4, HD * (j % 2)
        block = pl.ds(NEAR * r, NEAR)
        level = rm[j - j % 2 + 1, rows : rows + 1, :]
        before = m1[j, 0:1, block]
        newest = jnp.maximum(before, level)
        old, new = jnp.exp(before - newest), jnp.exp(level - newest)
        whole = o1[j, :, block]
        total = whole[HD : HD + 1] * old + new
        value = (whole[:HD] * old + rm[j - j % 2, rows : rows + HD, :] * new) * (1.0 / total)
        att[HD * j : HD * j + HD, block] = value.astype(BF16)

    pb[...] = jnp.zeros_like(pb)
    scores_of(0, 0, sa)
    level_ones(0, 6)
    arrived(T_SEND)
    start(T_FORWARD)
    arrived(T_SEND + 1, T_SEND + 2)
    start(T_FORWARD + 1, T_FORWARD + 2)
    level_ones(6, 10)
    arrived(*range(Q_SEND, Q_SEND + 7), T_SEND + 3, *range(T_FORWARD, T_FORWARD + 3), *range(X_SEND, X_SEND + 8))
    partials()
    start(*(R_SEND + slot - 1 for slot in (6, 2, 5, 7, 4, 1, 3)))
    arrived(L2_PAIR)
    start(L2_FWD)
    level_ones(10, 11)
    arrived(L2_PAIR + 1)
    start(L2_FWD + 1)
    level_ones(11, 12)
    mixed_of(HEADS - 1, 1, pb)
    spot = iota((ROWS, NEAR), 0)
    spot = (((spot & 255) >> 4) << 5) + (spot & 15) + ((1 - (spot >> 8)) << 4)
    index = ((spot & 3) << 7) + (((spot >> 2) & 7) << 4) + (((spot >> 5) & 7) << 1) + (spot >> 8)
    column = iota((ROWS, NEAR), 1)
    for c in range(4):
        back[:, NEAR * c : NEAR * c + NEAR] = one_hot(column + NEAR * c == index)
    arrived(L2_SIB, L2_FWD)
    level_two(0)
    arrived(L2_PAIR + 2)
    start(L2_FWD + 2)
    arrived(L2_FWD + 1)
    level_two(1)
    arrived(L2_PAIR + 3)
    start(L2_FWD + 3)
    arrived(L2_FWD + 2)
    level_two(2)
    arrived(L2_FWD + 3)
    level_two(3)
    for j in range(HEADS):
        block = pl.ds(NEAR * (j % 4), NEAR)
        whole = o1[j, :, block]
        att[HD * j : HD * j + HD, block] = (whole[:HD] * (1.0 / whole[HD : HD + 1])).astype(BF16)

    def project(part):
        natural = nt(back[256 * part : 256 * part + 256, :], att[...]).astype(BF16)
        rows = nn(natural, wbuf[...]).astype(BF16)
        for m in range(16):
            first = 32 * m + 16 - 16 * part
            out_ref[first : first + 16, :] = rows[16 * m : 16 * m + 16]

    loads[3].wait()
    project(0)
    arrived(*range(R_SEND, R_SEND + 7))
    merge_partials()
    for j in range(HEADS):
        finish(j)
    project(1)
    for number in range(COPIES):
        remote[number].wait_send()


def body(queries, keys, values, w_out):
    anywhere = pl.BlockSpec(memory_space=pltpu.HBM)
    scratch = [
        pltpu.VMEM((ROWS, D), BF16),
        pltpu.VMEM((ROWS, D), BF16),
        pltpu.VMEM((ROWS, D), BF16),
        pltpu.VMEM((D, D), BF16),
        pltpu.VMEM((ROWS, ROWS), BF16),
        pltpu.VMEM((ROWS, ROWS), BF16),
        pltpu.VMEM((HEADS, ROWS, WIDE), BF16),
        pltpu.VMEM((D, ROWS), BF16),
        pltpu.VMEM((8, HEADS, FAR, WIDE), BF16),
        pltpu.VMEM((4, HEADS, REST, WIDE), BF16),
        pltpu.VMEM((8, PAIRS, FAR, WIDE), BF16),
        pltpu.VMEM((2 * FAR, WIDE), BF16),
        pltpu.VMEM((8, 2 * FAR, WIDE), BF16),
        pltpu.VMEM((8, PAIRS + 1, FAR, WIDE), BF16),
        pltpu.VMEM((8, PAIRS + 1, FAR, WIDE), BF16),
        pltpu.VMEM((HEADS, WIDE, NEAR), F32),
        pltpu.VMEM((D, ROWS), BF16),
        pltpu.VMEM((ROWS, 256), F32),
        pltpu.VMEM((ROWS, 256), F32),
        pltpu.VMEM((ROWS, 256), BF16),
        pltpu.VMEM((ROWS, 256), BF16),
        pltpu.VMEM((HEADS, HD + FAR, ROWS), F32),
        pltpu.VMEM((HEADS, 8, ROWS), F32),
        pltpu.SemaphoreType.DMA((4,)),
        pltpu.SemaphoreType.DMA((COPIES,)),
        pltpu.SemaphoreType.DMA((COPIES,)),
    ]
    return pl.pallas_call(
        kernel,
        out_shape=jax.ShapeDtypeStruct((ROWS, D), BF16),
        in_specs=[anywhere] * 4,
        out_specs=pl.BlockSpec(memory_space=pltpu.VMEM),
        scratch_shapes=scratch,
        compiler_params=pltpu.CompilerParams(
            collective_id=0, has_side_effects=True, vmem_limit_bytes=53760 * 1024
        ),
        name="dilated_attention",
    )(queries, keys, values, w_out)


def solution(mesh):
    return jax.shard_map(
        body,
        mesh=mesh,
        in_specs=(P("seq", None), P("seq", None), P("seq", None), P()),
        out_specs=P("seq", None),
        check_vma=False,
    )
```

```python
import functools

import jax
import jax.numpy as jnp
from jax import lax
from jax.experimental import pallas as pl
from jax.experimental.pallas import tpu as pltpu
from jax.sharding import PartitionSpec as P

ROWS = 512
D = 768
HEADS = 12
HD = 64
GROUPS = 3
PAIRS = 6
NEAR = 128
FAR = 16
REST = NEAR - FAR
WIDE = 2 * HD
NONE = -1e30
F32 = jnp.float32
BF16 = jnp.bfloat16
MESH = pl.DeviceIdType.MESH


T_SEND = 0
T_FORWARD = 4
Q_SEND = 7
X_SEND = 14
R_SEND = 22
L2_SIB, L2_PAIR, L2_FWD = 29, 30, 33
COPIES = 36
CHUNKS = ((0, 2), (2, 4), (4, 6))


def nt(a, b):
    return lax.dot_general(a, b, (((1,), (1,)), ((), ())), preferred_element_type=F32)


def nn(a, b):
    return jnp.dot(a, b, preferred_element_type=F32)


def iota(shape, dim):
    return lax.broadcasted_iota(jnp.int32, shape, dim)


def one_hot(hit):
    return jnp.where(hit, 1.0, 0.0).astype(BF16)


def kernel(
    q_hbm, k_hbm, v_hbm, w_hbm, out_ref,
    qbuf, kbuf, vbuf, wbuf, pick, back, qp, vt, tg, kvr, qg, x4s, x4, rs, rg, rm, att, sa, sb, pa, pb, o1, m1,
    local_sem, send_sem, recv_sem,
):
    me = lax.axis_index("seq")
    zed = (me >> 3) & 3
    sib, pair = me ^ 1, me ^ 2
    base = me - (zed << 3)

    def around(slot):
        return (base + (((zed + slot) & 3) << 3)) ^ ((slot >> 2) << 5)

    def reverse(slot):
        return (slot & 4) + ((4 - slot) & 3)

    loads = []
    for number, (hbm, buf) in enumerate(((k_hbm, kbuf), (v_hbm, vbuf), (q_hbm, qbuf), (w_hbm, wbuf))):
        load = pltpu.make_async_copy(hbm, buf, local_sem.at[number])
        load.start()
        loads.append(load)
    barrier = pltpu.get_barrier_semaphore()
    peers = [sib] + [me ^ (2 * s) for s in (1, 2, 3)] + [around(s) for s in range(1, 8)] + [me ^ (96 + s) for s in range(8)]
    for peer in peers:
        pl.semaphore_signal(barrier, inc=1, device_id=(peer,), device_id_type=MESH)

    def copy(number, src, dst, device):
        return pltpu.make_async_remote_copy(
            src_ref=src, dst_ref=dst, send_sem=send_sem.at[number], recv_sem=recv_sem.at[number],
            device_id=(device,), device_id_type=MESH,
        )

    remote = {}
    for step, (mask, slot) in enumerate(((2, 1), (6, 4), (4, 5), (1, 2))):
        remote[T_SEND + step] = copy(T_SEND + step, tg.at[0], tg.at[slot], me ^ mask)
    for step, slot in enumerate((1, 4, 5)):
        remote[T_FORWARD + step] = copy(T_FORWARD + step, tg.at[slot], tg.at[slot + 2], sib)
    for slot in range(1, 8):
        number = slot - 1
        remote[Q_SEND + number] = copy(Q_SEND + number, qg.at[0], qg.at[reverse(slot)], around(slot))
        remote[R_SEND + number] = copy(R_SEND + number, rs.at[slot], rg.at[reverse(slot)], around(slot))
    for slot in range(8):
        remote[X_SEND + slot] = copy(X_SEND + slot, x4s, x4.at[slot], me ^ (96 + slot))
    remote[L2_SIB] = copy(L2_SIB, kvr.at[0], kvr.at[2], sib)
    for number, (first, last) in enumerate(CHUNKS):
        entries = pl.ds(2 * first, 2 * (last - first))
        remote[L2_PAIR + number] = copy(L2_PAIR + number, kvr.at[0, entries], kvr.at[1, entries], pair)
        remote[L2_FWD + number] = copy(L2_FWD + number, kvr.at[1, entries], kvr.at[3, entries], sib)

    def start(*numbers):
        for number in numbers:
            remote[number].start()

    def arrived(*numbers):
        for number in numbers:
            remote[number].wait_recv()

    place = iota((ROWS, NEAR), 0)
    position = ((place & 1) << 8) + (((place >> 1) & 7) << 5) + (((place >> 4) & 7) << 2) + (place >> 7)
    column = iota((ROWS, NEAR), 1)
    for c in range(4):
        pick[:, NEAR * c : NEAR * c + NEAR] = one_hot(column + NEAR * c == position)

    low_lanes = iota((NEAR, WIDE), 1) < HD

    loads[0].wait()
    loads[1].wait()
    for t in range(PAIRS):
        b, r = t // 2, 2 * (t % 2)
        columns = pl.ds(WIDE * t, WIDE)
        rows = pick[NEAR * r : NEAR * r + 2 * NEAR, :]
        both = nn(rows, jnp.concatenate((kbuf[:, columns], vbuf[:, columns]), axis=1))
        for kind in range(2):
            lanes = slice(WIDE * kind, WIDE * kind + WIDE)
            rows = jnp.where(low_lanes, both[:NEAR, lanes], both[NEAR:, lanes]).astype(BF16)
            tg[0, 2 * t + kind] = rows[FAR * b : FAR * b + FAR]
            if b > 0:
                kvr[0, 2 * t + kind, 0 : FAR * b, :] = rows[: FAR * b]
            kvr[0, 2 * t + kind, FAR * b : REST, :] = rows[FAR * b + FAR :]
    compact = iota((2 * FAR, HEADS * FAR), 0)
    compact = one_hot(iota((2 * FAR, HEADS * FAR), 1) == (compact >> 1) * FAR + (compact & 1))
    x4s[...] = nn(compact, tg[0].reshape(HEADS * FAR, WIDE)).astype(BF16)

    loads[2].wait()
    wide_low = iota((ROWS, WIDE), 1) < HD
    for b in range(GROUPS):
        ordered = nn(pick[...], qbuf[:, 256 * b : 256 * b + 256]) * 0.125
        for r in range(4):
            part = ordered[:, 128 * (r // 2) : 128 * (r // 2) + 128]
            whole = part[NEAR * r + FAR * b : NEAR * r + FAR * b + FAR]
            if r % 2 == 0:
                before = whole
            else:
                qg[0, 2 * b + r // 2] = jnp.where(low_lanes[:FAR], before, whole).astype(BF16)
            qp[4 * b + r] = jnp.where(wide_low, *((0.0, part) if r % 2 else (part, 0.0))).astype(BF16)
    eye = one_hot(iota((WIDE, WIDE), 0) == iota((WIDE, WIDE), 1))
    for t in range(PAIRS):
        vt[WIDE * t : WIDE * t + WIDE, :] = nt(eye, vbuf[:, WIDE * t : WIDE * t + WIDE]).astype(BF16)
    ones = jnp.ones((FAR, ROWS), BF16)

    pl.semaphore_wait(barrier, len(peers))
    start(*range(T_SEND, T_SEND + 3), *range(Q_SEND, Q_SEND + 7), *range(X_SEND, X_SEND + 8))
    start(*range(L2_PAIR, L2_PAIR + 3), T_SEND + 3, L2_SIB)


    def scores_of(j, part, into):
        columns = pl.ds(pl.multiple_of((j >> 1) * WIDE, WIDE), WIDE)
        span = pl.ds(256 * part, 256)
        queries = qp[j, span, :]
        highest = None
        for c in range(4):
            scores = nt(kbuf[NEAR * c : NEAR * c + NEAR, columns], queries)
            into[NEAR * c : NEAR * c + NEAR, :] = scores
            top = jnp.max(scores.reshape(16, 8, 256), axis=0)
            highest = top if highest is None else jnp.maximum(highest, top)
        m1[j, :, span] = jnp.broadcast_to(jnp.max(highest, axis=0, keepdims=True), (8, 256))

    def weights_of(j, part, scores, into):
        highest = m1[j, 0:1, 256 * part : 256 * part + 256]
        for c in range(4):
            rows = slice(NEAR * c, NEAR * c + NEAR)
            into[rows, :] = jnp.exp(scores[rows, :] - highest).astype(BF16)

    def mixed_of(j, part, weights):
        span = pl.ds(256 * part, 256)
        left = jnp.concatenate((vt[pl.ds(pl.multiple_of(j * HD, HD), HD), :], ones), axis=0)
        mixed = nn(left, weights[...])
        att[pl.ds(pl.multiple_of(j * HD, HD), HD), span] = (mixed[:HD] * (1.0 / mixed[HD : HD + 1])).astype(BF16)
        o1[j, :, span] = mixed

    def level_ones(first, last):
        def step(j, carry):
            weights_of(j, 0, sa, pa)
            scores_of(j, 1, sb)
            mixed_of(jnp.maximum(j - 1, 0), 1, pb)
            weights_of(j, 1, sb, pb)
            scores_of(jnp.minimum(j + 1, HEADS - 1), 0, sa)
            mixed_of(j, 0, pa)
            return carry

        lax.fori_loop(first, last, step, 0)

    def level_two(chunk):
        pairs = range(*CHUNKS[chunk])
        keys, lefts, highs = {}, {}, {}
        held = {t: ((sa, pa), (sb, pb))[t % 2] for t in pairs}

        def whole(entry):
            return jnp.concatenate(
                (tg[0:4, entry].reshape(4 * FAR, WIDE), kvr[0:4, entry].reshape(4 * REST, WIDE)), axis=0
            )

        def score(t):
            keys[t] = whole(2 * t)
            queries = [qp[j, NEAR * (j % 4) : NEAR * (j % 4) + NEAR, :] for j in (2 * t, 2 * t + 1)]
            queries = jnp.concatenate(queries, axis=0)
            highest = None
            for c in range(4):
                rows = slice(NEAR * c, NEAR * c + NEAR)
                scores = nt(keys[t][rows], queries)
                held[t][0][rows, :] = scores
                top = jnp.max(scores.reshape(16, 8, 256), axis=0)
                highest = top if highest is None else jnp.maximum(highest, top)
            highs[t] = jnp.max(highest, axis=0, keepdims=True)
            lefts[t] = jnp.concatenate((nt(eye, whole(2 * t + 1)).astype(BF16), ones), axis=0)

        def weigh(t):
            for c in range(4):
                rows = slice(NEAR * c, NEAR * c + NEAR)
                held[t][1][rows, :] = jnp.exp(held[t][0][rows, :] - highs[t]).astype(BF16)

        def mix(t):
            both = nn(lefts[t], held[t][1][...])
            for e in range(2):
                j = 2 * t + e
                lanes = slice(NEAR * e, NEAR * e + NEAR)
                mixed = jnp.concatenate((both[HD * e : HD * e + HD, lanes], both[WIDE:, lanes]), axis=0)
                highest = highs[t][:, lanes]
                block = pl.ds(NEAR * (j % 4), NEAR)
                before = m1[j, 0:1, block]
                newest = jnp.maximum(before, highest)
                o1[j, :, block] = o1[j, :, block] * jnp.exp(before - newest) + mixed * jnp.exp(highest - newest)
                m1[j, :, block] = jnp.broadcast_to(newest, (8, NEAR))

        pairs = list(pairs)
        for i in range(len(pairs) + 2):
            if i < len(pairs):
                score(pairs[i])
            if 0 <= i - 1 < len(pairs):
                weigh(pairs[i - 1])
            if 0 <= i - 2 < len(pairs):
                mix(pairs[i - 2])

    def partials():
        rows, near = 8 * FAR, (8 + 1) * FAR
        order = iota((HEADS * FAR, 8 * 2 * FAR), 0)
        column = iota((HEADS * FAR, 8 * 2 * FAR), 1)
        wanted = ((order & 15) >> 1) * 2 * FAR + (order >> 4) * 2 + (order & 1)
        other = nn(one_hot(column == wanted), x4[...].reshape(8 * 2 * FAR, WIDE)).astype(BF16)
        row, col = iota((near, 2 * rows), 0), iota((near, 2 * rows), 1)
        own_half = row < rows
        member = (col & 15) < 2
        bias = jnp.where(
            own_half,
            jnp.where(member & ((row & 15) < 2), 0.6931471805599453, 0.0),
            jnp.where(member, 0.0, NONE),
        ).astype(F32)
        low = (iota((rows, WIDE), 1) < HD).astype(F32)
        masks = (low.astype(BF16), (1.0 - low).astype(BF16))
        beside = jnp.ones((FAR, near), BF16)
        pairs, heads = range(PAIRS), range(HEADS)

        def whole(entry):
            return jnp.concatenate(
                (tg[:, entry].reshape(rows, WIDE), other[FAR * entry : FAR * entry + FAR]), axis=0
            )

        keys = [whole(2 * t) for t in pairs]
        lefts = [jnp.concatenate((nt(eye, whole(2 * t + 1)).astype(BF16), beside), axis=0) for t in pairs]
        queries = [qg[:, t].reshape(rows, WIDE) for t in pairs]
        queries = [jnp.concatenate((q * masks[0], q * masks[1]), axis=0) for q in queries]
        scores = [nt(keys[t], queries[t]) + bias for t in pairs]
        highest = [jnp.max(scores[t], axis=0, keepdims=True) for t in pairs]
        weights = [jnp.exp(scores[t] - highest[t]).astype(BF16) for t in pairs]
        mixed = [nn(lefts[t], weights[t]) for t in pairs]
        scales = [1.0 / mixed[t][WIDE : WIDE + 1] for t in pairs]
        both_levels = [highest[t] + jnp.log(mixed[t][WIDE : WIDE + 1]) for t in pairs]
        levels = [both_levels[j // 2][:, rows * (j % 2) : rows * (j % 2) + rows] for j in heads]
        values = [
            (
                mixed[j // 2][HD * (j % 2) : HD * (j % 2) + HD, rows * (j % 2) : rows * (j % 2) + rows]
                * scales[j // 2][:, rows * (j % 2) : rows * (j % 2) + rows]
            ).astype(BF16)
            for j in heads
        ]
        for t in pairs:
            both = jnp.concatenate((values[2 * t], values[2 * t + 1]), axis=0)
            rs[:, t] = nt(eye, both).astype(BF16).reshape(8, FAR, WIDE)
        levels = jnp.concatenate(levels + [jnp.zeros((4, rows), F32)], axis=0)
        coarse = levels.astype(BF16)
        fine = (levels - coarse.astype(F32)).astype(BF16)
        stacked = jnp.concatenate((coarse, fine, jnp.zeros((WIDE - 2 * FAR, rows), BF16)), axis=0)
        rs[:, PAIRS] = nt(eye, stacked).astype(BF16).reshape(8, FAR, WIDE)

    def merge_partials():
        source, lane = iota((WIDE, D), 0), iota((WIDE, D), 1)
        gather = one_hot(((source & 15) == (lane >> 6)) & (source < 2 * FAR))
        rs_own = rs[0]
        tiles = [rs_own] + [rg[slot] for slot in range(1, 8)]
        values = [jnp.concatenate([tile[t] for t in range(PAIRS)], axis=1).astype(F32) for tile in tiles]
        levels = nn(jnp.concatenate([tile[PAIRS] for tile in tiles], axis=0), gather)
        levels = [levels[FAR * slot : FAR * slot + FAR] for slot in range(8)]
        highest = functools.reduce(jnp.maximum, levels)
        factors = [jnp.exp(level - highest) for level in levels]
        total = functools.reduce(jnp.add, factors)
        value = functools.reduce(jnp.add, [f * v for f, v in zip(factors, values)]) / total
        level = highest + jnp.log(total)
        coarse = level.astype(BF16)
        fine = (level - coarse.astype(F32)).astype(BF16)
        value = value.astype(BF16)
        column = iota((WIDE, NEAR), 1)
        for t in range(PAIRS):
            b = t // 2
            lanes = slice(WIDE * t, WIDE * t + WIDE)

            def spread(rows):
                empty = jnp.zeros((REST, WIDE), BF16)
                rows = (rows, empty) if b == 0 else (empty[: FAR * b], rows, empty[FAR * b :])
                return nt(eye, jnp.concatenate(rows, axis=0))

            rm[2 * t] = spread(value[:, lanes])
            rm[2 * t + 1] = jnp.where(
                (column >> 4) == b, spread(coarse[:, lanes]) + spread(fine[:, lanes]), NONE
            )

    def finish(j):
        r, rows = j % 4, HD * (j % 2)
        block = pl.ds(NEAR * r, NEAR)
        level = rm[j - j % 2 + 1, rows : rows + 1, :]
        before = m1[j, 0:1, block]
        newest = jnp.maximum(before, level)
        old, new = jnp.exp(before - newest), jnp.exp(level - newest)
        whole = o1[j, :, block]
        total = whole[HD : HD + 1] * old + new
        value = (whole[:HD] * old + rm[j - j % 2, rows : rows + HD, :] * new) * (1.0 / total)
        att[HD * j : HD * j + HD, block] = value.astype(BF16)

    pb[...] = jnp.zeros_like(pb)
    scores_of(0, 0, sa)
    level_ones(0, 6)
    arrived(T_SEND)
    start(T_FORWARD)
    arrived(T_SEND + 1, T_SEND + 2)
    start(T_FORWARD + 1, T_FORWARD + 2)
    level_ones(6, 10)
    arrived(*range(Q_SEND, Q_SEND + 7), T_SEND + 3, *range(T_FORWARD, T_FORWARD + 3), *range(X_SEND, X_SEND + 8))
    partials()
    start(*(R_SEND + slot - 1 for slot in (6, 2, 5, 7, 4, 1, 3)))
    arrived(L2_PAIR)
    start(L2_FWD)
    level_ones(10, 11)
    arrived(L2_PAIR + 1)
    start(L2_FWD + 1)
    level_ones(11, 12)
    mixed_of(HEADS - 1, 1, pb)
    spot = iota((ROWS, NEAR), 0)
    spot = (((spot & 255) >> 4) << 5) + (spot & 15) + ((1 - (spot >> 8)) << 4)
    index = ((spot & 3) << 7) + (((spot >> 2) & 7) << 4) + (((spot >> 5) & 7) << 1) + (spot >> 8)
    column = iota((ROWS, NEAR), 1)
    for c in range(4):
        back[:, NEAR * c : NEAR * c + NEAR] = one_hot(column + NEAR * c == index)
    arrived(L2_SIB, L2_FWD)
    level_two(0)
    arrived(L2_PAIR + 2)
    start(L2_FWD + 2)
    arrived(L2_FWD + 1)
    level_two(1)
    arrived(L2_FWD + 2)
    level_two(2)
    for j in range(HEADS):
        block = pl.ds(NEAR * (j % 4), NEAR)
        whole = o1[j, :, block]
        att[HD * j : HD * j + HD, block] = (whole[:HD] * (1.0 / whole[HD : HD + 1])).astype(BF16)

    def project(part):
        natural = nt(back[256 * part : 256 * part + 256, :], att[...]).astype(BF16)
        rows = nn(natural, wbuf[...]).astype(BF16)
        for m in range(16):
            first = 32 * m + 16 - 16 * part
            out_ref[first : first + 16, :] = rows[16 * m : 16 * m + 16]

    loads[3].wait()
    project(0)
    arrived(*range(R_SEND, R_SEND + 7))
    merge_partials()
    for j in range(HEADS):
        finish(j)
    project(1)
    for number in range(COPIES):
        remote[number].wait_send()


def body(queries, keys, values, w_out):
    anywhere = pl.BlockSpec(memory_space=pltpu.HBM)
    scratch = [
        pltpu.VMEM((ROWS, D), BF16),
        pltpu.VMEM((ROWS, D), BF16),
        pltpu.VMEM((ROWS, D), BF16),
        pltpu.VMEM((D, D), BF16),
        pltpu.VMEM((ROWS, ROWS), BF16),
        pltpu.VMEM((ROWS, ROWS), BF16),
        pltpu.VMEM((HEADS, ROWS, WIDE), BF16),
        pltpu.VMEM((D, ROWS), BF16),
        pltpu.VMEM((8, HEADS, FAR, WIDE), BF16),
        pltpu.VMEM((4, HEADS, REST, WIDE), BF16),
        pltpu.VMEM((8, PAIRS, FAR, WIDE), BF16),
        pltpu.VMEM((2 * FAR, WIDE), BF16),
        pltpu.VMEM((8, 2 * FAR, WIDE), BF16),
        pltpu.VMEM((8, PAIRS + 1, FAR, WIDE), BF16),
        pltpu.VMEM((8, PAIRS + 1, FAR, WIDE), BF16),
        pltpu.VMEM((HEADS, WIDE, NEAR), F32),
        pltpu.VMEM((D, ROWS), BF16),
        pltpu.VMEM((ROWS, 256), F32),
        pltpu.VMEM((ROWS, 256), F32),
        pltpu.VMEM((ROWS, 256), BF16),
        pltpu.VMEM((ROWS, 256), BF16),
        pltpu.VMEM((HEADS, HD + FAR, ROWS), F32),
        pltpu.VMEM((HEADS, 8, ROWS), F32),
        pltpu.SemaphoreType.DMA((4,)),
        pltpu.SemaphoreType.DMA((COPIES,)),
        pltpu.SemaphoreType.DMA((COPIES,)),
    ]
    return pl.pallas_call(
        kernel,
        out_shape=jax.ShapeDtypeStruct((ROWS, D), BF16),
        in_specs=[anywhere] * 4,
        out_specs=pl.BlockSpec(memory_space=pltpu.VMEM),
        scratch_shapes=scratch,
        compiler_params=pltpu.CompilerParams(
            collective_id=0, has_side_effects=True, vmem_limit_bytes=53760 * 1024
        ),
        name="dilated_attention",
    )(queries, keys, values, w_out)


def solution(mesh):
    return jax.shard_map(
        body,
        mesh=mesh,
        in_specs=(P("seq", None), P("seq", None), P("seq", None), P()),
        out_specs=P("seq", None),
        check_vma=False,
    )
```

```python
import functools

import jax
import jax.numpy as jnp
from jax import lax
from jax.experimental import pallas as pl
from jax.experimental.pallas import tpu as pltpu
from jax.sharding import PartitionSpec as P

ROWS = 512
D = 768
HEADS = 12
HD = 64
GROUPS = 3
PAIRS = 6
NEAR = 128
FAR = 16
REST = NEAR - FAR
WIDE = 2 * HD
NONE = -1e30
F32 = jnp.float32
BF16 = jnp.bfloat16
MESH = pl.DeviceIdType.MESH


T_SEND = 0
T_FORWARD = 4
Q_SEND = 7
X_SEND = 14
R_SEND = 22
L2_SIB, L2_PAIR, L2_FWD = 29, 30, 33
COPIES = 36
CHUNKS = ((0, 2), (2, 4), (4, 6))


def nt(a, b):
    return lax.dot_general(a, b, (((1,), (1,)), ((), ())), preferred_element_type=F32)


def nn(a, b):
    return jnp.dot(a, b, preferred_element_type=F32)


def iota(shape, dim):
    return lax.broadcasted_iota(jnp.int32, shape, dim)


def one_hot(hit):
    return jnp.where(hit, 1.0, 0.0).astype(BF16)


def kernel(
    q_hbm, k_hbm, v_hbm, w_hbm, out_ref,
    qbuf, kbuf, vbuf, wbuf, pick, back, qp, vt, tg, kvr, qg, x4s, x4, rs, rg, rm, att, sa, sb, pa, pb, o1, m1,
    local_sem, send_sem, recv_sem,
):
    me = lax.axis_index("seq")
    zed = (me >> 3) & 3
    sib, pair = me ^ 1, me ^ 2
    base = me - (zed << 3)

    def around(slot):
        return (base + (((zed + slot) & 3) << 3)) ^ ((slot >> 2) << 5)

    def reverse(slot):
        return (slot & 4) + ((4 - slot) & 3)

    loads = []
    for number, (hbm, buf) in enumerate(((k_hbm, kbuf), (v_hbm, vbuf), (q_hbm, qbuf), (w_hbm, wbuf))):
        load = pltpu.make_async_copy(hbm, buf, local_sem.at[number])
        load.start()
        loads.append(load)
    barrier = pltpu.get_barrier_semaphore()
    peers = [sib] + [me ^ (2 * s) for s in (1, 2, 3)] + [around(s) for s in range(1, 8)] + [me ^ (96 + s) for s in range(8)]
    for peer in peers:
        pl.semaphore_signal(barrier, inc=1, device_id=(peer,), device_id_type=MESH)

    def copy(number, src, dst, device):
        return pltpu.make_async_remote_copy(
            src_ref=src, dst_ref=dst, send_sem=send_sem.at[number], recv_sem=recv_sem.at[number],
            device_id=(device,), device_id_type=MESH,
        )

    remote = {}
    for step, (mask, slot) in enumerate(((2, 1), (6, 4), (4, 5), (1, 2))):
        remote[T_SEND + step] = copy(T_SEND + step, tg.at[0], tg.at[slot], me ^ mask)
    for step, slot in enumerate((1, 4, 5)):
        remote[T_FORWARD + step] = copy(T_FORWARD + step, tg.at[slot], tg.at[slot + 2], sib)
    for slot in range(1, 8):
        number = slot - 1
        remote[Q_SEND + number] = copy(Q_SEND + number, qg.at[0], qg.at[reverse(slot)], around(slot))
        remote[R_SEND + number] = copy(R_SEND + number, rs.at[slot], rg.at[reverse(slot)], around(slot))
    for slot in range(8):
        remote[X_SEND + slot] = copy(X_SEND + slot, x4s, x4.at[slot], me ^ (96 + slot))
    remote[L2_SIB] = copy(L2_SIB, kvr.at[0], kvr.at[2], sib)
    for number, (first, last) in enumerate(CHUNKS):
        entries = pl.ds(2 * first, 2 * (last - first))
        remote[L2_PAIR + number] = copy(L2_PAIR + number, kvr.at[0, entries], kvr.at[1, entries], pair)
        remote[L2_FWD + number] = copy(L2_FWD + number, kvr.at[1, entries], kvr.at[3, entries], sib)

    def start(*numbers):
        for number in numbers:
            remote[number].start()

    def arrived(*numbers):
        for number in numbers:
            remote[number].wait_recv()

    place = iota((ROWS, NEAR), 0)
    position = ((place & 1) << 8) + (((place >> 1) & 7) << 5) + (((place >> 4) & 7) << 2) + (place >> 7)
    column = iota((ROWS, NEAR), 1)
    for c in range(4):
        pick[:, NEAR * c : NEAR * c + NEAR] = one_hot(column + NEAR * c == position)

    low_lanes = iota((NEAR, WIDE), 1) < HD

    loads[0].wait()
    loads[1].wait()
    for t in range(PAIRS):
        b, r = t // 2, 2 * (t % 2)
        columns = pl.ds(WIDE * t, WIDE)
        rows = pick[NEAR * r : NEAR * r + 2 * NEAR, :]
        both = nn(rows, jnp.concatenate((kbuf[:, columns], vbuf[:, columns]), axis=1))
        for kind in range(2):
            lanes = slice(WIDE * kind, WIDE * kind + WIDE)
            rows = jnp.where(low_lanes, both[:NEAR, lanes], both[NEAR:, lanes]).astype(BF16)
            tg[0, 2 * t + kind] = rows[FAR * b : FAR * b + FAR]
            if b > 0:
                kvr[0, 2 * t + kind, 0 : FAR * b, :] = rows[: FAR * b]
            kvr[0, 2 * t + kind, FAR * b : REST, :] = rows[FAR * b + FAR :]
    compact = iota((2 * FAR, HEADS * FAR), 0)
    compact = one_hot(iota((2 * FAR, HEADS * FAR), 1) == (compact >> 1) * FAR + (compact & 1))
    x4s[...] = nn(compact, tg[0].reshape(HEADS * FAR, WIDE)).astype(BF16)

    loads[2].wait()
    wide_low = iota((ROWS, WIDE), 1) < HD
    for b in range(GROUPS):
        ordered = nn(pick[...], qbuf[:, 256 * b : 256 * b + 256]) * 0.125
        for r in range(4):
            part = ordered[:, 128 * (r // 2) : 128 * (r // 2) + 128]
            whole = part[NEAR * r + FAR * b : NEAR * r + FAR * b + FAR]
            if r % 2 == 0:
                before = whole
            else:
                qg[0, 2 * b + r // 2] = jnp.where(low_lanes[:FAR], before, whole).astype(BF16)
            qp[4 * b + r] = jnp.where(wide_low, *((0.0, part) if r % 2 else (part, 0.0))).astype(BF16)
    eye = one_hot(iota((WIDE, WIDE), 0) == iota((WIDE, WIDE), 1))
    for t in range(PAIRS):
        vt[WIDE * t : WIDE * t + WIDE, :] = nt(eye, vbuf[:, WIDE * t : WIDE * t + WIDE]).astype(BF16)
    ones = jnp.ones((FAR, ROWS), BF16)

    pl.semaphore_wait(barrier, len(peers))
    start(*range(T_SEND, T_SEND + 3), *range(Q_SEND, Q_SEND + 7), *range(X_SEND, X_SEND + 8))
    start(*range(L2_PAIR, L2_PAIR + 3), T_SEND + 3, L2_SIB)


    def scores_of(j, part, into):
        columns = pl.ds(pl.multiple_of((j >> 1) * WIDE, WIDE), WIDE)
        span = pl.ds(256 * part, 256)
        queries = qp[j, span, :]
        highest = None
        for c in range(4):
            scores = nt(kbuf[NEAR * c : NEAR * c + NEAR, columns], queries)
            into[NEAR * c : NEAR * c + NEAR, :] = scores
            top = jnp.max(scores.reshape(16, 8, 256), axis=0)
            highest = top if highest is None else jnp.maximum(highest, top)
        m1[j, :, span] = jnp.broadcast_to(jnp.max(highest, axis=0, keepdims=True), (8, 256))

    def weights_of(j, part, scores, into):
        highest = m1[j, 0:1, 256 * part : 256 * part + 256]
        for c in range(4):
            rows = slice(NEAR * c, NEAR * c + NEAR)
            into[rows, :] = jnp.exp(scores[rows, :] - highest).astype(BF16)

    def mixed_of(j, part, weights):
        span = pl.ds(256 * part, 256)
        left = jnp.concatenate((vt[pl.ds(pl.multiple_of(j * HD, HD), HD), :], ones), axis=0)
        mixed = nn(left, weights[...])
        att[pl.ds(pl.multiple_of(j * HD, HD), HD), span] = (mixed[:HD] * (1.0 / mixed[HD : HD + 1])).astype(BF16)
        o1[j, :, span] = mixed

    def level_ones(first, last):
        def step(j, carry):
            weights_of(j, 0, sa, pa)
            scores_of(j, 1, sb)
            mixed_of(jnp.maximum(j - 1, 0), 1, pb)
            weights_of(j, 1, sb, pb)
            scores_of(jnp.minimum(j + 1, HEADS - 1), 0, sa)
            mixed_of(j, 0, pa)
            return carry

        lax.fori_loop(first, last, step, 0)

    def level_two(chunk):
        pairs = range(*CHUNKS[chunk])
        keys, lefts, highs = {}, {}, {}
        held = {t: ((sa, pa), (sb, pb))[t % 2] for t in pairs}

        def whole(entry):
            return jnp.concatenate(
                (tg[0:4, entry].reshape(4 * FAR, WIDE), kvr[0:4, entry].reshape(4 * REST, WIDE)), axis=0
            )

        def score(t):
            keys[t] = whole(2 * t)
            queries = [qp[j, NEAR * (j % 4) : NEAR * (j % 4) + NEAR, :] for j in (2 * t, 2 * t + 1)]
            queries = jnp.concatenate(queries, axis=0)
            highest = None
            for c in range(4):
                rows = slice(NEAR * c, NEAR * c + NEAR)
                scores = nt(keys[t][rows], queries)
                held[t][0][rows, :] = scores
                top = jnp.max(scores.reshape(16, 8, 256), axis=0)
                highest = top if highest is None else jnp.maximum(highest, top)
            highs[t] = jnp.max(highest, axis=0, keepdims=True)
            lefts[t] = jnp.concatenate((nt(eye, whole(2 * t + 1)).astype(BF16), ones), axis=0)

        def weigh(t):
            for c in range(4):
                rows = slice(NEAR * c, NEAR * c + NEAR)
                held[t][1][rows, :] = jnp.exp(held[t][0][rows, :] - highs[t]).astype(BF16)

        def mix(t):
            both = nn(lefts[t], held[t][1][...])
            for e in range(2):
                j = 2 * t + e
                lanes = slice(NEAR * e, NEAR * e + NEAR)
                mixed = jnp.concatenate((both[HD * e : HD * e + HD, lanes], both[WIDE:, lanes]), axis=0)
                highest = highs[t][:, lanes]
                block = pl.ds(NEAR * (j % 4), NEAR)
                before = m1[j, 0:1, block]
                newest = jnp.maximum(before, highest)
                o1[j, :, block] = o1[j, :, block] * jnp.exp(before - newest) + mixed * jnp.exp(highest - newest)
                m1[j, :, block] = jnp.broadcast_to(newest, (8, NEAR))

        pairs = list(pairs)
        for i in range(len(pairs) + 2):
            if i < len(pairs):
                score(pairs[i])
            if 0 <= i - 1 < len(pairs):
                weigh(pairs[i - 1])
            if 0 <= i - 2 < len(pairs):
                mix(pairs[i - 2])

    def partial_constants():
        rows, near = 8 * FAR, (8 + 1) * FAR
        order = iota((HEADS * FAR, 8 * 2 * FAR), 0)
        column = iota((HEADS * FAR, 8 * 2 * FAR), 1)
        wanted = ((order & 15) >> 1) * 2 * FAR + (order >> 4) * 2 + (order & 1)
        row, col = iota((near, 2 * rows), 0), iota((near, 2 * rows), 1)
        own_half = row < rows
        member = (col & 15) < 2
        bias = jnp.where(
            own_half,
            jnp.where(member & ((row & 15) < 2), 0.6931471805599453, 0.0),
            jnp.where(member, 0.0, NONE),
        ).astype(F32)
        low = (iota((rows, WIDE), 1) < HD).astype(F32)
        masks = (low.astype(BF16), (1.0 - low).astype(BF16))
        beside = jnp.ones((FAR, near), BF16)
        return one_hot(column == wanted), bias, masks, beside

    def partials(wanted, bias, masks, beside):
        rows = 8 * FAR
        other = nn(wanted, x4[...].reshape(8 * 2 * FAR, WIDE)).astype(BF16)
        pairs, heads = range(PAIRS), range(HEADS)

        def whole(entry):
            return jnp.concatenate(
                (tg[:, entry].reshape(rows, WIDE), other[FAR * entry : FAR * entry + FAR]), axis=0
            )

        keys = [whole(2 * t) for t in pairs]
        lefts = [jnp.concatenate((nt(eye, whole(2 * t + 1)).astype(BF16), beside), axis=0) for t in pairs]
        queries = [qg[:, t].reshape(rows, WIDE) for t in pairs]
        queries = [jnp.concatenate((q * masks[0], q * masks[1]), axis=0) for q in queries]
        scores = [nt(keys[t], queries[t]) + bias for t in pairs]
        highest = [jnp.max(scores[t], axis=0, keepdims=True) for t in pairs]
        weights = [jnp.exp(scores[t] - highest[t]).astype(BF16) for t in pairs]
        mixed = [nn(lefts[t], weights[t]) for t in pairs]
        scales = [1.0 / mixed[t][WIDE : WIDE + 1] for t in pairs]
        both_levels = [highest[t] + jnp.log(mixed[t][WIDE : WIDE + 1]) for t in pairs]
        levels = [both_levels[j // 2][:, rows * (j % 2) : rows * (j % 2) + rows] for j in heads]
        values = [
            (
                mixed[j // 2][HD * (j % 2) : HD * (j % 2) + HD, rows * (j % 2) : rows * (j % 2) + rows]
                * scales[j // 2][:, rows * (j % 2) : rows * (j % 2) + rows]
            ).astype(BF16)
            for j in heads
        ]
        for t in pairs:
            both = jnp.concatenate((values[2 * t], values[2 * t + 1]), axis=0)
            rs[:, t] = nt(eye, both).astype(BF16).reshape(8, FAR, WIDE)
        levels = jnp.concatenate(levels + [jnp.zeros((4, rows), F32)], axis=0)
        coarse = levels.astype(BF16)
        fine = (levels - coarse.astype(F32)).astype(BF16)
        stacked = jnp.concatenate((coarse, fine, jnp.zeros((WIDE - 2 * FAR, rows), BF16)), axis=0)
        rs[:, PAIRS] = nt(eye, stacked).astype(BF16).reshape(8, FAR, WIDE)

    def level_lanes():
        source, lane = iota((WIDE, D), 0), iota((WIDE, D), 1)
        return one_hot(((source & 15) == (lane >> 6)) & (source < 2 * FAR))

    def merge_partials(gather, member):
        rs_own = rs[0]
        tiles = [rs_own] + [rg[slot] for slot in range(1, 8)]
        values = [jnp.concatenate([tile[t] for t in range(PAIRS)], axis=1).astype(F32) for tile in tiles]
        levels = nn(jnp.concatenate([tile[PAIRS] for tile in tiles], axis=0), gather)
        levels = [levels[FAR * slot : FAR * slot + FAR] for slot in range(8)]
        highest = functools.reduce(jnp.maximum, levels)
        factors = [jnp.exp(level - highest) for level in levels]
        total = functools.reduce(jnp.add, factors)
        value = functools.reduce(jnp.add, [f * v for f, v in zip(factors, values)]) / total
        level = highest + jnp.log(total)
        coarse = level.astype(BF16)
        fine = (level - coarse.astype(F32)).astype(BF16)
        value = value.astype(BF16)
        empty = jnp.zeros((REST, WIDE), BF16)
        for t in range(PAIRS):
            b = t // 2
            stack = []
            for part in (value, coarse, fine):
                part = part[:, WIDE * t : WIDE * t + WIDE]
                stack += (part, empty) if b == 0 else (empty[: FAR * b], part, empty[FAR * b :])
            spread = nt(eye, jnp.concatenate(stack, axis=0))
            rm[2 * t] = spread[:, :NEAR]
            rm[2 * t + 1] = jnp.where(member == b, spread[:, NEAR : 2 * NEAR] + spread[:, 2 * NEAR :], NONE)

    def finish(j):
        r, rows = j % 4, HD * (j % 2)
        block = pl.ds(NEAR * r, NEAR)
        level = rm[j - j % 2 + 1, rows : rows + 1, :]
        before = m1[j, 0:1, block]
        newest = jnp.maximum(before, level)
        old, new = jnp.exp(before - newest), jnp.exp(level - newest)
        whole = o1[j, :, block]
        total = whole[HD : HD + 1] * old + new
        value = (whole[:HD] * old + rm[j - j % 2, rows : rows + HD, :] * new) * (1.0 / total)
        att[HD * j : HD * j + HD, block] = value.astype(BF16)

    pb[...] = jnp.zeros_like(pb)
    scores_of(0, 0, sa)
    level_ones(0, 6)
    arrived(T_SEND)
    start(T_FORWARD)
    arrived(T_SEND + 1, T_SEND + 2)
    start(T_FORWARD + 1, T_FORWARD + 2)
    level_ones(6, 11)
    spot = iota((ROWS, NEAR), 0)
    spot = (((spot & 255) >> 4) << 5) + (spot & 15) + ((1 - (spot >> 8)) << 4)
    index = ((spot & 3) << 7) + (((spot >> 2) & 7) << 4) + (((spot >> 5) & 7) << 1) + (spot >> 8)
    column = iota((ROWS, NEAR), 1)
    for c in range(4):
        back[:, NEAR * c : NEAR * c + NEAR] = one_hot(column + NEAR * c == index)
    constants = partial_constants()
    arrived(*range(Q_SEND, Q_SEND + 7), T_SEND + 3, *range(T_FORWARD, T_FORWARD + 3), *range(X_SEND, X_SEND + 8))
    partials(*constants)
    start(*(R_SEND + slot - 1 for slot in (6, 2, 5, 7, 4, 1, 3)))
    arrived(L2_PAIR)
    start(L2_FWD)
    arrived(L2_PAIR + 1)
    start(L2_FWD + 1)
    level_ones(11, 12)
    mixed_of(HEADS - 1, 1, pb)
    arrived(L2_SIB, L2_FWD)
    level_two(0)
    arrived(L2_PAIR + 2)
    start(L2_FWD + 2)
    arrived(L2_FWD + 1)
    level_two(1)
    arrived(L2_FWD + 2)
    level_two(2)
    for j in range(HEADS):
        block = pl.ds(NEAR * (j % 4), NEAR)
        whole = o1[j, :, block]
        att[HD * j : HD * j + HD, block] = (whole[:HD] * (1.0 / whole[HD : HD + 1])).astype(BF16)

    def project(part):
        natural = nt(back[256 * part : 256 * part + 256, :], att[...]).astype(BF16)
        rows = nn(natural, wbuf[...]).astype(BF16)
        for m in range(16):
            first = 32 * m + 16 - 16 * part
            out_ref[first : first + 16, :] = rows[16 * m : 16 * m + 16]

    loads[3].wait()
    project(0)
    gather, member = level_lanes(), iota((WIDE, NEAR), 1) >> 4
    arrived(*range(R_SEND, R_SEND + 7))
    merge_partials(gather, member)
    for j in range(HEADS):
        finish(j)
    project(1)
    for number in range(COPIES):
        remote[number].wait_send()


def body(queries, keys, values, w_out):
    anywhere = pl.BlockSpec(memory_space=pltpu.HBM)
    scratch = [
        pltpu.VMEM((ROWS, D), BF16),
        pltpu.VMEM((ROWS, D), BF16),
        pltpu.VMEM((ROWS, D), BF16),
        pltpu.VMEM((D, D), BF16),
        pltpu.VMEM((ROWS, ROWS), BF16),
        pltpu.VMEM((ROWS, ROWS), BF16),
        pltpu.VMEM((HEADS, ROWS, WIDE), BF16),
        pltpu.VMEM((D, ROWS), BF16),
        pltpu.VMEM((8, HEADS, FAR, WIDE), BF16),
        pltpu.VMEM((4, HEADS, REST, WIDE), BF16),
        pltpu.VMEM((8, PAIRS, FAR, WIDE), BF16),
        pltpu.VMEM((2 * FAR, WIDE), BF16),
        pltpu.VMEM((8, 2 * FAR, WIDE), BF16),
        pltpu.VMEM((8, PAIRS + 1, FAR, WIDE), BF16),
        pltpu.VMEM((8, PAIRS + 1, FAR, WIDE), BF16),
        pltpu.VMEM((HEADS, WIDE, NEAR), F32),
        pltpu.VMEM((D, ROWS), BF16),
        pltpu.VMEM((ROWS, 256), F32),
        pltpu.VMEM((ROWS, 256), F32),
        pltpu.VMEM((ROWS, 256), BF16),
        pltpu.VMEM((ROWS, 256), BF16),
        pltpu.VMEM((HEADS, HD + FAR, ROWS), F32),
        pltpu.VMEM((HEADS, 8, ROWS), F32),
        pltpu.SemaphoreType.DMA((4,)),
        pltpu.SemaphoreType.DMA((COPIES,)),
        pltpu.SemaphoreType.DMA((COPIES,)),
    ]
    return pl.pallas_call(
        kernel,
        out_shape=jax.ShapeDtypeStruct((ROWS, D), BF16),
        in_specs=[anywhere] * 4,
        out_specs=pl.BlockSpec(memory_space=pltpu.VMEM),
        scratch_shapes=scratch,
        compiler_params=pltpu.CompilerParams(
            collective_id=0, has_side_effects=True, vmem_limit_bytes=53760 * 1024
        ),
        name="dilated_attention",
    )(queries, keys, values, w_out)


def solution(mesh):
    return jax.shard_map(
        body,
        mesh=mesh,
        in_specs=(P("seq", None), P("seq", None), P("seq", None), P()),
        out_specs=P("seq", None),
        check_vma=False,
    )
```

```python
import functools

import jax
import jax.numpy as jnp
from jax import lax
from jax.experimental import pallas as pl
from jax.experimental.pallas import tpu as pltpu
from jax.sharding import PartitionSpec as P

ROWS = 512
D = 768
HEADS = 12
HD = 64
GROUPS = 3
PAIRS = 6
NEAR = 128
FAR = 16
REST = NEAR - FAR
WIDE = 2 * HD
NONE = -1e30
F32 = jnp.float32
BF16 = jnp.bfloat16
MESH = pl.DeviceIdType.MESH


T_SEND = 0
T_FORWARD = 4
Q_SEND = 7
X_SEND = 14
R_SEND = 22
L2_SIB, L2_PAIR, L2_FWD = 29, 30, 33
COPIES = 36
CHUNKS = ((0, 2), (2, 4), (4, 6))


def nt(a, b):
    return lax.dot_general(a, b, (((1,), (1,)), ((), ())), preferred_element_type=F32)


def nn(a, b):
    return jnp.dot(a, b, preferred_element_type=F32)


def iota(shape, dim):
    return lax.broadcasted_iota(jnp.int32, shape, dim)


def one_hot(hit):
    return jnp.where(hit, 1.0, 0.0).astype(BF16)


def kernel(
    q_hbm, k_hbm, v_hbm, w_hbm, out_ref,
    qbuf, kbuf, vbuf, wbuf, pick, back, qp, vt, tg, kvr, qg, x4s, x4, rs, rg, rm, att, sa, sb, pa, pb, o1, m1,
    local_sem, send_sem, recv_sem,
):
    me = lax.axis_index("seq")
    zed = (me >> 3) & 3
    sib, pair = me ^ 1, me ^ 2
    base = me - (zed << 3)

    def around(slot):
        return (base + (((zed + slot) & 3) << 3)) ^ ((slot >> 2) << 5)

    def reverse(slot):
        return (slot & 4) + ((4 - slot) & 3)

    loads = []
    for number, (hbm, buf) in enumerate(((k_hbm, kbuf), (v_hbm, vbuf), (q_hbm, qbuf), (w_hbm, wbuf))):
        load = pltpu.make_async_copy(hbm, buf, local_sem.at[number])
        load.start()
        loads.append(load)
    barrier = pltpu.get_barrier_semaphore()
    peers = [sib] + [me ^ (2 * s) for s in (1, 2, 3)] + [around(s) for s in range(1, 8)] + [me ^ (96 + s) for s in range(8)]
    for peer in peers:
        pl.semaphore_signal(barrier, inc=1, device_id=(peer,), device_id_type=MESH)

    def copy(number, src, dst, device):
        return pltpu.make_async_remote_copy(
            src_ref=src, dst_ref=dst, send_sem=send_sem.at[number], recv_sem=recv_sem.at[number],
            device_id=(device,), device_id_type=MESH,
        )

    remote = {}
    for step, (mask, slot) in enumerate(((2, 1), (6, 4), (4, 5), (1, 2))):
        remote[T_SEND + step] = copy(T_SEND + step, tg.at[0], tg.at[slot], me ^ mask)
    for step, slot in enumerate((1, 4, 5)):
        remote[T_FORWARD + step] = copy(T_FORWARD + step, tg.at[slot], tg.at[slot + 2], sib)
    for slot in range(1, 8):
        number = slot - 1
        remote[Q_SEND + number] = copy(Q_SEND + number, qg.at[0], qg.at[reverse(slot)], around(slot))
        remote[R_SEND + number] = copy(R_SEND + number, rs.at[slot], rg.at[reverse(slot)], around(slot))
    for slot in range(8):
        remote[X_SEND + slot] = copy(X_SEND + slot, x4s, x4.at[slot], me ^ (96 + slot))
    remote[L2_SIB] = copy(L2_SIB, kvr.at[0], kvr.at[2], sib)
    for number, (first, last) in enumerate(CHUNKS):
        entries = pl.ds(2 * first, 2 * (last - first))
        remote[L2_PAIR + number] = copy(L2_PAIR + number, kvr.at[0, entries], kvr.at[1, entries], pair)
        remote[L2_FWD + number] = copy(L2_FWD + number, kvr.at[1, entries], kvr.at[3, entries], sib)

    def start(*numbers):
        for number in numbers:
            remote[number].start()

    def arrived(*numbers):
        for number in numbers:
            remote[number].wait_recv()

    place = iota((ROWS, NEAR), 0)
    position = ((place & 1) << 8) + (((place >> 1) & 7) << 5) + (((place >> 4) & 7) << 2) + (place >> 7)
    column = iota((ROWS, NEAR), 1)
    for c in range(4):
        pick[:, NEAR * c : NEAR * c + NEAR] = one_hot(column + NEAR * c == position)

    low_lanes = iota((NEAR, WIDE), 1) < HD

    loads[0].wait()
    loads[1].wait()
    for t in range(PAIRS):
        b, r = t // 2, 2 * (t % 2)
        columns = pl.ds(WIDE * t, WIDE)
        rows = pick[NEAR * r : NEAR * r + 2 * NEAR, :]
        both = nn(rows, jnp.concatenate((kbuf[:, columns], vbuf[:, columns]), axis=1))
        for kind in range(2):
            lanes = slice(WIDE * kind, WIDE * kind + WIDE)
            rows = jnp.where(low_lanes, both[:NEAR, lanes], both[NEAR:, lanes]).astype(BF16)
            tg[0, 2 * t + kind] = rows[FAR * b : FAR * b + FAR]
            if b > 0:
                kvr[0, 2 * t + kind, 0 : FAR * b, :] = rows[: FAR * b]
            kvr[0, 2 * t + kind, FAR * b : REST, :] = rows[FAR * b + FAR :]
    compact = iota((2 * FAR, HEADS * FAR), 0)
    compact = one_hot(iota((2 * FAR, HEADS * FAR), 1) == (compact >> 1) * FAR + (compact & 1))
    x4s[...] = nn(compact, tg[0].reshape(HEADS * FAR, WIDE)).astype(BF16)

    loads[2].wait()
    wide_low = iota((ROWS, WIDE), 1) < HD
    for b in range(GROUPS):
        ordered = nn(pick[...], qbuf[:, 256 * b : 256 * b + 256]) * 0.125
        for r in range(4):
            part = ordered[:, 128 * (r // 2) : 128 * (r // 2) + 128]
            whole = part[NEAR * r + FAR * b : NEAR * r + FAR * b + FAR]
            if r % 2 == 0:
                before = whole
            else:
                qg[0, 2 * b + r // 2] = jnp.where(low_lanes[:FAR], before, whole).astype(BF16)
            qp[4 * b + r] = jnp.where(wide_low, *((0.0, part) if r % 2 else (part, 0.0))).astype(BF16)
    eye = one_hot(iota((WIDE, WIDE), 0) == iota((WIDE, WIDE), 1))
    pl.semaphore_wait(barrier, len(peers))
    start(*range(T_SEND, T_SEND + 3), *range(Q_SEND, Q_SEND + 7), *range(X_SEND, X_SEND + 8))
    start(*range(L2_PAIR, L2_PAIR + 3), T_SEND + 3, L2_SIB)


    for t in range(PAIRS):
        vt[WIDE * t : WIDE * t + WIDE, :] = nt(eye, vbuf[:, WIDE * t : WIDE * t + WIDE]).astype(BF16)
    ones = jnp.ones((FAR, ROWS), BF16)

    def scores_of(j, part, into):
        columns = pl.ds(pl.multiple_of((j >> 1) * WIDE, WIDE), WIDE)
        span = pl.ds(256 * part, 256)
        queries = qp[j, span, :]
        highest = None
        for c in range(4):
            scores = nt(kbuf[NEAR * c : NEAR * c + NEAR, columns], queries)
            into[NEAR * c : NEAR * c + NEAR, :] = scores
            top = jnp.max(scores.reshape(16, 8, 256), axis=0)
            highest = top if highest is None else jnp.maximum(highest, top)
        m1[j, :, span] = jnp.broadcast_to(jnp.max(highest, axis=0, keepdims=True), (8, 256))

    def weights_of(j, part, scores, into):
        highest = m1[j, 0:1, 256 * part : 256 * part + 256]
        for c in range(4):
            rows = slice(NEAR * c, NEAR * c + NEAR)
            into[rows, :] = jnp.exp(scores[rows, :] - highest).astype(BF16)

    def mixed_of(j, part, weights):
        span = pl.ds(256 * part, 256)
        left = jnp.concatenate((vt[pl.ds(pl.multiple_of(j * HD, HD), HD), :], ones), axis=0)
        mixed = nn(left, weights[...])
        att[pl.ds(pl.multiple_of(j * HD, HD), HD), span] = (mixed[:HD] * (1.0 / mixed[HD : HD + 1])).astype(BF16)
        o1[j, :, span] = mixed

    def level_ones(first, last):
        def step(j, carry):
            weights_of(j, 0, sa, pa)
            scores_of(j, 1, sb)
            mixed_of(jnp.maximum(j - 1, 0), 1, pb)
            weights_of(j, 1, sb, pb)
            scores_of(jnp.minimum(j + 1, HEADS - 1), 0, sa)
            mixed_of(j, 0, pa)
            return carry

        lax.fori_loop(first, last, step, 0)

    def level_two(chunk):
        pairs = range(*CHUNKS[chunk])
        keys, lefts, highs = {}, {}, {}
        held = {t: ((sa, pa), (sb, pb))[t % 2] for t in pairs}

        def whole(entry):
            return jnp.concatenate(
                (tg[0:4, entry].reshape(4 * FAR, WIDE), kvr[0:4, entry].reshape(4 * REST, WIDE)), axis=0
            )

        def score(t):
            keys[t] = whole(2 * t)
            queries = [qp[j, NEAR * (j % 4) : NEAR * (j % 4) + NEAR, :] for j in (2 * t, 2 * t + 1)]
            queries = jnp.concatenate(queries, axis=0)
            highest = None
            for c in range(4):
                rows = slice(NEAR * c, NEAR * c + NEAR)
                scores = nt(keys[t][rows], queries)
                held[t][0][rows, :] = scores
                top = jnp.max(scores.reshape(16, 8, 256), axis=0)
                highest = top if highest is None else jnp.maximum(highest, top)
            highs[t] = jnp.max(highest, axis=0, keepdims=True)
            lefts[t] = jnp.concatenate((nt(eye, whole(2 * t + 1)).astype(BF16), ones), axis=0)

        def weigh(t):
            for c in range(4):
                rows = slice(NEAR * c, NEAR * c + NEAR)
                held[t][1][rows, :] = jnp.exp(held[t][0][rows, :] - highs[t]).astype(BF16)

        def mix(t):
            both = nn(lefts[t], held[t][1][...])
            for e in range(2):
                j = 2 * t + e
                lanes = slice(NEAR * e, NEAR * e + NEAR)
                mixed = jnp.concatenate((both[HD * e : HD * e + HD, lanes], both[WIDE:, lanes]), axis=0)
                highest = highs[t][:, lanes]
                block = pl.ds(NEAR * (j % 4), NEAR)
                before = m1[j, 0:1, block]
                newest = jnp.maximum(before, highest)
                o1[j, :, block] = o1[j, :, block] * jnp.exp(before - newest) + mixed * jnp.exp(highest - newest)
                m1[j, :, block] = jnp.broadcast_to(newest, (8, NEAR))

        pairs = list(pairs)
        for i in range(len(pairs) + 2):
            if i < len(pairs):
                score(pairs[i])
            if 0 <= i - 1 < len(pairs):
                weigh(pairs[i - 1])
            if 0 <= i - 2 < len(pairs):
                mix(pairs[i - 2])

    def partial_constants():
        rows, near = 8 * FAR, (8 + 1) * FAR
        order = iota((HEADS * FAR, 8 * 2 * FAR), 0)
        column = iota((HEADS * FAR, 8 * 2 * FAR), 1)
        wanted = ((order & 15) >> 1) * 2 * FAR + (order >> 4) * 2 + (order & 1)
        row, col = iota((near, 2 * rows), 0), iota((near, 2 * rows), 1)
        own_half = row < rows
        member = (col & 15) < 2
        bias = jnp.where(
            own_half,
            jnp.where(member & ((row & 15) < 2), 0.6931471805599453, 0.0),
            jnp.where(member, 0.0, NONE),
        ).astype(F32)
        low = (iota((rows, WIDE), 1) < HD).astype(F32)
        masks = (low.astype(BF16), (1.0 - low).astype(BF16))
        beside = jnp.ones((FAR, near), BF16)
        return one_hot(column == wanted), bias, masks, beside

    def partials(wanted, bias, masks, beside):
        rows = 8 * FAR
        other = nn(wanted, x4[...].reshape(8 * 2 * FAR, WIDE)).astype(BF16)
        pairs, heads = range(PAIRS), range(HEADS)

        def whole(entry):
            return jnp.concatenate(
                (tg[:, entry].reshape(rows, WIDE), other[FAR * entry : FAR * entry + FAR]), axis=0
            )

        keys = [whole(2 * t) for t in pairs]
        lefts = [jnp.concatenate((nt(eye, whole(2 * t + 1)).astype(BF16), beside), axis=0) for t in pairs]
        queries = [qg[:, t].reshape(rows, WIDE) for t in pairs]
        queries = [jnp.concatenate((q * masks[0], q * masks[1]), axis=0) for q in queries]
        scores = [nt(keys[t], queries[t]) + bias for t in pairs]
        highest = [jnp.max(scores[t], axis=0, keepdims=True) for t in pairs]
        weights = [jnp.exp(scores[t] - highest[t]).astype(BF16) for t in pairs]
        mixed = [nn(lefts[t], weights[t]) for t in pairs]
        scales = [1.0 / mixed[t][WIDE : WIDE + 1] for t in pairs]
        both_levels = [highest[t] + jnp.log(mixed[t][WIDE : WIDE + 1]) for t in pairs]
        levels = [both_levels[j // 2][:, rows * (j % 2) : rows * (j % 2) + rows] for j in heads]
        values = [
            (
                mixed[j // 2][HD * (j % 2) : HD * (j % 2) + HD, rows * (j % 2) : rows * (j % 2) + rows]
                * scales[j // 2][:, rows * (j % 2) : rows * (j % 2) + rows]
            ).astype(BF16)
            for j in heads
        ]
        for t in pairs:
            both = jnp.concatenate((values[2 * t], values[2 * t + 1]), axis=0)
            rs[:, t] = nt(eye, both).astype(BF16).reshape(8, FAR, WIDE)
        levels = jnp.concatenate(levels + [jnp.zeros((4, rows), F32)], axis=0)
        coarse = levels.astype(BF16)
        fine = (levels - coarse.astype(F32)).astype(BF16)
        stacked = jnp.concatenate((coarse, fine, jnp.zeros((WIDE - 2 * FAR, rows), BF16)), axis=0)
        rs[:, PAIRS] = nt(eye, stacked).astype(BF16).reshape(8, FAR, WIDE)

    def level_lanes():
        source, lane = iota((WIDE, D), 0), iota((WIDE, D), 1)
        return one_hot(((source & 15) == (lane >> 6)) & (source < 2 * FAR))

    def merge_partials(gather, member):
        rs_own = rs[0]
        tiles = [rs_own] + [rg[slot] for slot in range(1, 8)]
        values = [jnp.concatenate([tile[t] for t in range(PAIRS)], axis=1).astype(F32) for tile in tiles]
        levels = nn(jnp.concatenate([tile[PAIRS] for tile in tiles], axis=0), gather)
        levels = [levels[FAR * slot : FAR * slot + FAR] for slot in range(8)]
        highest = functools.reduce(jnp.maximum, levels)
        factors = [jnp.exp(level - highest) for level in levels]
        total = functools.reduce(jnp.add, factors)
        value = functools.reduce(jnp.add, [f * v for f, v in zip(factors, values)]) / total
        level = highest + jnp.log(total)
        coarse = level.astype(BF16)
        fine = (level - coarse.astype(F32)).astype(BF16)
        value = value.astype(BF16)
        empty = jnp.zeros((REST, WIDE), BF16)
        for t in range(PAIRS):
            b = t // 2
            stack = []
            for part in (value, coarse, fine):
                part = part[:, WIDE * t : WIDE * t + WIDE]
                stack += (part, empty) if b == 0 else (empty[: FAR * b], part, empty[FAR * b :])
            spread = nt(eye, jnp.concatenate(stack, axis=0))
            rm[2 * t] = spread[:, :NEAR]
            rm[2 * t + 1] = jnp.where(member == b, spread[:, NEAR : 2 * NEAR] + spread[:, 2 * NEAR :], NONE)

    def finish(j):
        r, rows = j % 4, HD * (j % 2)
        block = pl.ds(NEAR * r, NEAR)
        level = rm[j - j % 2 + 1, rows : rows + 1, :]
        before = m1[j, 0:1, block]
        newest = jnp.maximum(before, level)
        old, new = jnp.exp(before - newest), jnp.exp(level - newest)
        whole = o1[j, :, block]
        total = whole[HD : HD + 1] * old + new
        value = (whole[:HD] * old + rm[j - j % 2, rows : rows + HD, :] * new) * (1.0 / total)
        att[HD * j : HD * j + HD, block] = value.astype(BF16)

    pb[...] = jnp.zeros_like(pb)
    scores_of(0, 0, sa)
    level_ones(0, 6)
    arrived(T_SEND)
    start(T_FORWARD)
    arrived(T_SEND + 1, T_SEND + 2)
    start(T_FORWARD + 1, T_FORWARD + 2)
    level_ones(6, 11)
    spot = iota((ROWS, NEAR), 0)
    spot = (((spot & 255) >> 4) << 5) + (spot & 15) + ((1 - (spot >> 8)) << 4)
    index = ((spot & 3) << 7) + (((spot >> 2) & 7) << 4) + (((spot >> 5) & 7) << 1) + (spot >> 8)
    column = iota((ROWS, NEAR), 1)
    for c in range(4):
        back[:, NEAR * c : NEAR * c + NEAR] = one_hot(column + NEAR * c == index)
    constants = partial_constants()
    arrived(*range(Q_SEND, Q_SEND + 7), T_SEND + 3, *range(T_FORWARD, T_FORWARD + 3), *range(X_SEND, X_SEND + 8))
    partials(*constants)
    start(*(R_SEND + slot - 1 for slot in (6, 2, 5, 7, 4, 1, 3)))
    arrived(L2_PAIR)
    start(L2_FWD)
    arrived(L2_PAIR + 1)
    start(L2_FWD + 1)
    level_ones(11, 12)
    mixed_of(HEADS - 1, 1, pb)
    arrived(L2_SIB, L2_FWD)
    level_two(0)
    arrived(L2_PAIR + 2)
    start(L2_FWD + 2)
    arrived(L2_FWD + 1)
    level_two(1)
    arrived(L2_FWD + 2)
    level_two(2)
    for j in range(HEADS):
        block = pl.ds(NEAR * (j % 4), NEAR)
        whole = o1[j, :, block]
        att[HD * j : HD * j + HD, block] = (whole[:HD] * (1.0 / whole[HD : HD + 1])).astype(BF16)

    def project(part):
        natural = nt(back[256 * part : 256 * part + 256, :], att[...]).astype(BF16)
        rows = nn(natural, wbuf[...]).astype(BF16)
        for m in range(16):
            first = 32 * m + 16 - 16 * part
            out_ref[first : first + 16, :] = rows[16 * m : 16 * m + 16]

    loads[3].wait()
    project(0)
    gather, member = level_lanes(), iota((WIDE, NEAR), 1) >> 4
    arrived(*range(R_SEND, R_SEND + 7))
    merge_partials(gather, member)
    for j in range(HEADS):
        finish(j)
    project(1)
    for number in range(COPIES):
        remote[number].wait_send()


def body(queries, keys, values, w_out):
    anywhere = pl.BlockSpec(memory_space=pltpu.HBM)
    scratch = [
        pltpu.VMEM((ROWS, D), BF16),
        pltpu.VMEM((ROWS, D), BF16),
        pltpu.VMEM((ROWS, D), BF16),
        pltpu.VMEM((D, D), BF16),
        pltpu.VMEM((ROWS, ROWS), BF16),
        pltpu.VMEM((ROWS, ROWS), BF16),
        pltpu.VMEM((HEADS, ROWS, WIDE), BF16),
        pltpu.VMEM((D, ROWS), BF16),
        pltpu.VMEM((8, HEADS, FAR, WIDE), BF16),
        pltpu.VMEM((4, HEADS, REST, WIDE), BF16),
        pltpu.VMEM((8, PAIRS, FAR, WIDE), BF16),
        pltpu.VMEM((2 * FAR, WIDE), BF16),
        pltpu.VMEM((8, 2 * FAR, WIDE), BF16),
        pltpu.VMEM((8, PAIRS + 1, FAR, WIDE), BF16),
        pltpu.VMEM((8, PAIRS + 1, FAR, WIDE), BF16),
        pltpu.VMEM((HEADS, WIDE, NEAR), F32),
        pltpu.VMEM((D, ROWS), BF16),
        pltpu.VMEM((ROWS, 256), F32),
        pltpu.VMEM((ROWS, 256), F32),
        pltpu.VMEM((ROWS, 256), BF16),
        pltpu.VMEM((ROWS, 256), BF16),
        pltpu.VMEM((HEADS, HD + FAR, ROWS), F32),
        pltpu.VMEM((HEADS, 8, ROWS), F32),
        pltpu.SemaphoreType.DMA((4,)),
        pltpu.SemaphoreType.DMA((COPIES,)),
        pltpu.SemaphoreType.DMA((COPIES,)),
    ]
    return pl.pallas_call(
        kernel,
        out_shape=jax.ShapeDtypeStruct((ROWS, D), BF16),
        in_specs=[anywhere] * 4,
        out_specs=pl.BlockSpec(memory_space=pltpu.VMEM),
        scratch_shapes=scratch,
        compiler_params=pltpu.CompilerParams(
            collective_id=0, has_side_effects=True, vmem_limit_bytes=53760 * 1024
        ),
        name="dilated_attention",
    )(queries, keys, values, w_out)


def solution(mesh):
    return jax.shard_map(
        body,
        mesh=mesh,
        in_specs=(P("seq", None), P("seq", None), P("seq", None), P()),
        out_specs=P("seq", None),
        check_vma=False,
    )
```
